128 devices in a mesh: branch: 16 (over z_hi, x, core), seq: 8 (over z_lo, y).
Axes of the slice: x: 4, y: 4, z: 4 (z_hi: 2, z_lo: 2; z = z_hi * 2 + z_lo), core: 2. Of those that a mesh axis runs over, the one named last changes fastest.
Arguments:
- frame_tokens: bfloat16 [32, 256, 5120], P('branch', 'seq'), may hold values from -6 to 6
- actions: int32 [32], P('branch'), may hold values from 0 to 15
- visible_from: int32 [32], P('branch'), may hold values from 0 to 16
- action_modulation_table: bfloat16 [16, 3, 5120], replicated, may hold values from -3 to 3
- w_qkv: bfloat16 [5120, 3, 3072], P(None, None, 'seq'), may hold values from -0.078125 to 0.078125
- w_out: bfloat16 [3072, 5120], P('seq'), may hold values from -0.109375 to 0.109375
- ctx_kv: bfloat16 [2, 8192, 3072], P(None, 'branch', 'seq'), may hold values from -400 to 400
Outputs:
- layer_out: bfloat16 [32, 256, 5120], P('branch', 'seq')
The draws below stay inside these ranges and needn't reach their ends.
Inputs may be any that keep to these rules, and one draw needn't show every extreme that they name: Branch b attends to the context frames visible_from[b] to 31 and always to its own frame.
All inputs are finite; a program needn't handle non-finite values.
Results may differ from the reference program's by a relative error of at most 0.0085.
Values may be sent and summed in bfloat16 or wider, within the bound.
No kernel may reach another device: no remote copies, remote signals or barrier semaphores. Data moves between devices by JAX's collectives and lax.ppermute only.
A program may use at most 128 MiB of HBM per device.

```python
import jax
import jax.numpy as jnp
from jax import lax

D = 5120
HEADS = 24
HDIM = 128
ACTIONS = 16
FRAME_TOK = 256
BRANCHES = 32
CTX_FRAMES = 32
CTX_TOK = 8192
N_SEQ = 8


def draw_ctx_kv(key, part):
    key = jax.random.fold_in(key, 7)
    key_base = jax.random.fold_in(key, 0)
    shape = (2, CTX_TOK, HEADS * HDIM)
    return jnp.clip(jax.random.normal(key_base, shape, jnp.float32), -6.0, 6.0).astype(jnp.bfloat16)


def plant(entries, rng, smallest, largest):
    spot = [jax.random.randint(jax.random.fold_in(rng, axis), (), 0, length) for axis, length in enumerate(entries.shape)]
    widest = entries.shape.index(max(entries.shape))
    next_to = spot[:widest] + [(spot[widest] + 1) % entries.shape[widest]] + spot[widest + 1:]
    return entries.at[tuple(spot)].set(smallest).at[tuple(next_to)].set(largest)


def block_levels(own_key, shape, cuts, low, high):
    def one(axis_at, blocks):
        draws = jax.random.uniform(jax.random.fold_in(jax.random.fold_in(own_key, 6), axis_at), (blocks,), jnp.float32, low / len(cuts), high / len(cuts))
        return jnp.repeat(jnp.exp(draws), shape[axis_at] // blocks).reshape((-1,) + (1,) * (len(shape) - axis_at - 1))

    loudness = one(*cuts[0])
    for cut in cuts[1:]:
        loudness = loudness * one(*cut)
    return loudness


def noise(rng, shape, deviation, reach, shards=(), kind=jnp.bfloat16):
    drawn = deviation * jax.random.normal(rng, shape, jnp.float32)
    if shards:
        drawn = drawn * block_levels(rng, shape, shards, -0.22, 0.18)
    return jnp.clip(drawn, -reach, reach).astype(kind)


def setup_inputs(seed: int = 0) -> dict:
    streams_of = jax.random.split(jax.random.key(seed), 8)
    return {
        "frame_tokens": noise(streams_of[0], (BRANCHES, FRAME_TOK, D), 1.0, 6.0, ((0, 16), (1, 8))),
        "actions": plant(jax.random.randint(streams_of[1], (BRANCHES,), 0, ACTIONS), jax.random.fold_in(streams_of[1], 1), 0, ACTIONS - 1).astype(jnp.int32),
        "visible_from": plant(jax.random.randint(streams_of[2], (BRANCHES,), 0, CTX_FRAMES // 2 + 1), jax.random.fold_in(streams_of[2], 1), 0, (CTX_FRAMES // 2 + 1) - 1).astype(jnp.int32),
        "action_modulation_table": noise(streams_of[3], (ACTIONS, 3, D), 0.5, 3.0),
        "w_qkv": noise(streams_of[4], (D, 3, HEADS * HDIM), D ** -0.5, 0.078125, ((2, 8),)),
        "w_out": noise(streams_of[5], (HEADS * HDIM, D), (HEADS * HDIM) ** -0.5, 0.109375, ((0, 8),)),
        "ctx_kv": draw_ctx_kv(jax.random.fold_in(streams_of[7], 71), 0),
    }


def layer_norm(value_rows):
    value_rows = value_rows.astype(jnp.float32)
    mean = lax.optimization_barrier(jnp.mean(value_rows, axis=-1, keepdims=True))
    centred = value_rows - mean
    variance = lax.optimization_barrier(jnp.mean(centred * centred, axis=-1, keepdims=True))
    return centred / jnp.sqrt(variance + 1e-06)

def reference(frame_tokens, actions, visible_from, action_modulation_table, w_qkv, w_out, ctx_kv):
    scale = HDIM ** (-0.5)
    action_indicator = (actions[:, None] == jnp.arange(ACTIONS, dtype=jnp.int32)[None, :]).astype(jnp.float32)
    action_shift_scale = jnp.einsum('wn,nlg->wlg', action_indicator, action_modulation_table.astype(jnp.float32))
    context_frame_index = jnp.arange(CTX_TOK, dtype=jnp.int32) // FRAME_TOK
    ctx_keys = ctx_kv[0].astype(jnp.float32).reshape(CTX_TOK, HEADS, HDIM)
    ctx_vals = ctx_kv[1].astype(jnp.float32).reshape(CTX_TOK, HEADS, HDIM)
    weights_qkv = w_qkv.astype(jnp.float32)
    group = HEADS * HDIM // N_SEQ
    out_rows = w_out.astype(jnp.float32)

    def branch_step(item):
        tokens, modul, start = item
        hidden = (layer_norm(tokens) * (1.0 + modul[1]) + modul[0]).astype(jnp.bfloat16)
        qkv = jnp.einsum('td,dkh->tkh', hidden.astype(jnp.float32), weights_qkv).astype(jnp.bfloat16)
        qkv = lax.optimization_barrier(qkv).astype(jnp.float32)
        queries = qkv[:, 0].reshape(FRAME_TOK, HEADS, HDIM)
        keys = jnp.concatenate([ctx_keys, qkv[:, 1].reshape(FRAME_TOK, HEADS, HDIM)], axis=0)
        vals = jnp.concatenate([ctx_vals, qkv[:, 2].reshape(FRAME_TOK, HEADS, HDIM)], axis=0)
        valid = jnp.concatenate([context_frame_index >= start, jnp.ones((FRAME_TOK,), bool)])
        attention_logits = jnp.einsum('qhd,khd->hqk', queries, keys) * scale
        attention_logits = jnp.where(valid[None, None, :], attention_logits, -1e+30)
        top = lax.optimization_barrier(jnp.max(attention_logits, axis=-1, keepdims=True))
        expo = jnp.where(valid[None, None, :], jnp.exp(attention_logits - top), 0.0)
        total = lax.optimization_barrier(jnp.sum(expo, axis=-1))
        probs = lax.optimization_barrier(expo.astype(jnp.bfloat16)).astype(jnp.float32)
        summed = jnp.einsum('hqk,khd->qhd', probs, vals) / jnp.transpose(total)[:, :, None]
        attended = summed.astype(jnp.bfloat16).reshape(FRAME_TOK, HEADS * HDIM).astype(jnp.float32)
        projected = jnp.zeros((FRAME_TOK, D), jnp.float32)
        for index in range(N_SEQ):
            partial_value = jnp.dot(attended[:, index * group:(index + 1) * group], out_rows[index * group:(index + 1) * group])
            projected = projected + partial_value.astype(jnp.bfloat16).astype(jnp.float32)
        return (tokens.astype(jnp.float32) + modul[2] * projected).astype(jnp.bfloat16)
    return lax.map(branch_step, (frame_tokens, action_shift_scale, visible_from))
```

```python
import functools
import math

import jax
import jax.numpy as jnp
from jax import lax
from jax.experimental import pallas as pl
from jax.experimental.pallas import tpu as pltpu
from jax.sharding import PartitionSpec as P

HDIM = 128
ACTIONS = 16
FRAME_TOK = 256
HERE = 3
WIDTH = HERE * HDIM
SCALE2 = math.log2(math.e) * HDIM ** (-0.5)
MASKED = -1e30
VMEM = pl.BlockSpec(memory_space=pltpu.VMEM)
SMEM = pl.BlockSpec(memory_space=pltpu.SMEM)
ANY = pl.BlockSpec(memory_space=pl.ANY)


def along_seq(a, dy=0, dz=0):
    perm = [
        (z * 4 + y, (z + dz) % 2 * 4 + (y + dy) % 4) for z in range(2) for y in range(4)
    ]
    return lax.ppermute(a, "seq", perm)


def along_branch(a, dx=0, dz=0, dc=0):
    perm = [
        ((z * 4 + x) * 2 + c, ((z + dz) % 2 * 4 + (x + dx) % 4) * 2 + (c + dc) % 2)
        for z in range(2)
        for x in range(4)
        for c in range(2)
    ]
    return lax.ppermute(a, "branch", perm)


def across_z(a):
    perm = []
    for b in range(16):
        for s in range(8):
            perm.append((b * 8 + s, (b + 8) % 16 * 8 + (s + 4) % 8))
    return lax.ppermute(a, ("branch", "seq"), perm)


def norm_kernel(actions, x_ref, table_ref, hidden_ref, gate_ref):
    rows = lax.broadcasted_iota(jnp.int32, (ACTIONS, 1), 0)
    for b in range(x_ref.shape[0]):
        pick = rows == actions[b]
        shift, scale, gate = (
            jnp.sum(
                jnp.where(pick, table_ref[c].astype(jnp.float32), 0.0), axis=0, keepdims=True
            )
            for c in range(3)
        )
        gate_ref[b] = gate
        x = x_ref[b].astype(jnp.float32)
        centred = x - jnp.mean(x, axis=-1, keepdims=True)
        variance = jnp.mean(centred * centred, axis=-1, keepdims=True)
        normed = centred * (1.0 / jnp.sqrt(variance + 1e-06))
        hidden_ref[b] = (normed * (1.0 + scale) + shift).astype(jnp.bfloat16)


def norm(actions, x, table):
    return pl.pallas_call(
        norm_kernel,
        out_shape=(
            jax.ShapeDtypeStruct(x.shape, jnp.bfloat16),
            jax.ShapeDtypeStruct((x.shape[0], 1, x.shape[2]), jnp.float32),
        ),
        in_specs=[SMEM, VMEM, VMEM],
        out_specs=(VMEM, VMEM),
        compiler_params=pltpu.CompilerParams(vmem_limit_bytes=24 << 20),
    )(actions, x, table)


def qkv_kernel(count, *refs):
    shards, w_ref, outs, acc = refs[:count], refs[count], refs[count + 1 : count + 4], refs[-1]
    step = pl.program_id(0)
    x = jnp.concatenate([s[b] for b in range(2) for s in shards], axis=0)

    @pl.when(step == 0)
    def _():
        acc[...] = jnp.zeros_like(acc)

    for c in range(3):
        acc[c] += jnp.dot(x, w_ref[c], preferred_element_type=jnp.float32)

    @pl.when(step == pl.num_programs(0) - 1)
    def _():
        rows = count * 32
        for c in range(3):
            for b in range(2):
                outs[c][b] = acc[c, b * rows : (b + 1) * rows].astype(jnp.bfloat16)


def project_qkv(shards, w):
    count, depth, block = len(shards), w.shape[1], 1024
    rows = count * 32
    out = jax.ShapeDtypeStruct((2, rows, WIDTH), jnp.bfloat16)
    return pl.pallas_call(
        functools.partial(qkv_kernel, count),
        grid=(depth // block,),
        out_shape=(out,) * 3,
        in_specs=[pl.BlockSpec((2, 32, block), lambda i: (0, 0, i))] * count
        + [pl.BlockSpec((3, block, WIDTH), lambda i: (0, i, 0))],
        out_specs=(pl.BlockSpec((2, rows, WIDTH), lambda i: (0, 0, 0)),) * 3,
        scratch_shapes=[pltpu.VMEM((3, 2 * rows, WIDTH), jnp.float32)],
        compiler_params=pltpu.CompilerParams(vmem_limit_bytes=32 << 20),
        cost_estimate=pl.CostEstimate(
            flops=2 * 2 * rows * depth * 3 * WIDTH,
            bytes_accessed=depth * 3 * WIDTH * 2 + 2 * rows * depth * 2,
            transcendentals=0,
        ),
    )(*shards, w)


def attend_kernel(branches, chunk, blocks, own, start_ref, q_ref, frame_ref, *rest):
    if own:
        own_k, own_v, rest = rest[0], rest[1], rest[2:]
    parts, o_ref, stat_ref, kv, top_s, sum_s, acc_s, sems = rest[:blocks], *rest[blocks:]
    copies = [
        pltpu.make_async_copy(parts[i], kv.at[:, pl.ds(i * 512, 512)], sems.at[i])
        for i in range(blocks)
    ]
    for copy in copies:
        copy.start()

    def block_step(b, h, k, v, bias, first):
        q = q_ref[b, :, h * HDIM : (h + 1) * HDIM]
        s = lax.dot_general(q, k, (((1,), (1,)), ((), ())), preferred_element_type=jnp.float32)
        s = s * SCALE2
        if bias is not None:
            s = s + bias
        top = jnp.max(s, axis=1, keepdims=True)
        if first:
            new = jnp.broadcast_to(top, (FRAME_TOK, HDIM))
        else:
            old = top_s[b, h]
            new = jnp.maximum(old, top)
        p = jnp.exp2(s - new[:, :1])
        sums = p[:, :HDIM]
        for j in range(1, p.shape[1] // HDIM):
            sums = sums + p[:, j * HDIM : (j + 1) * HDIM]
        pv = jnp.dot(p.astype(jnp.bfloat16), v, preferred_element_type=jnp.float32)
        if first:
            sum_s[b, h] = sums
            acc_s[b, h] = pv
        else:
            factor = jnp.exp2(old - new)
            sum_s[b, h] = sum_s[b, h] * factor + sums
            acc_s[b, h] = acc_s[b, h] * factor + pv
        top_s[b, h] = new

    if own:
        for b in range(branches):
            for h in range(HERE):
                cols = slice(h * HDIM, (h + 1) * HDIM)
                block_step(b, h, own_k[b, :, cols], own_v[b, :, cols], None, True)
    else:
        top_s[...] = jnp.full_like(top_s[...], 2 * MASKED)
        sum_s[...] = jnp.zeros_like(sum_s[...])
        acc_s[...] = jnp.zeros_like(acc_s[...])
    for copy in copies:
        copy.wait()

    def loop(i, _):
        rows = pl.ds(pl.multiple_of(i * chunk, chunk), chunk)
        for b in range(branches):
            bias = jnp.where(frame_ref[pl.ds(i, 1), :] >= start_ref[b], 0.0, MASKED)
            for h in range(HERE):
                cols = slice(h * HDIM, (h + 1) * HDIM)
                block_step(b, h, kv[0, rows, cols], kv[1, rows, cols], bias, False)
        return 0

    lax.fori_loop(0, blocks * 512 // chunk, loop, 0)
    lane = lax.broadcasted_iota(jnp.int32, (FRAME_TOK, HDIM), 1)
    for b in range(branches):
        stats = jnp.zeros((FRAME_TOK, HDIM), jnp.float32)
        for h in range(HERE):
            total = jnp.sum(sum_s[b, h], axis=1, keepdims=True)
            o_ref[b, :, h * HDIM : (h + 1) * HDIM] = (acc_s[b, h] / total).astype(o_ref.dtype)
            left = top_s[b, h] + jnp.log2(total)
            for part in range(3):
                piece = left.astype(jnp.bfloat16).astype(jnp.float32)
                stats = jnp.where(lane == h * 3 + part, piece, stats)
                left = left - piece
        stat_ref[b] = stats.astype(jnp.bfloat16)


def attend(start, q, frames, parts, own=None, dtype=jnp.bfloat16):
    branches, blocks, chunk = q.shape[0], len(parts), 2048
    state = pltpu.VMEM((branches, HERE, FRAME_TOK, HDIM), jnp.float32)
    return pl.pallas_call(
        functools.partial(attend_kernel, branches, chunk, blocks, own is not None),
        out_shape=(
            jax.ShapeDtypeStruct((branches, FRAME_TOK, WIDTH), dtype),
            jax.ShapeDtypeStruct((branches, FRAME_TOK, HDIM), jnp.bfloat16),
        ),
        in_specs=[SMEM, VMEM, VMEM] + ([VMEM, VMEM] if own else []) + [ANY] * blocks,
        out_specs=(VMEM, VMEM),
        scratch_shapes=[
            pltpu.VMEM((2, blocks * 512, WIDTH), jnp.bfloat16),
            state,
            state,
            state,
            pltpu.SemaphoreType.DMA((blocks,)),
        ],
        compiler_params=pltpu.CompilerParams(vmem_limit_bytes=40 << 20),
        cost_estimate=pl.CostEstimate(
            flops=8 * branches * FRAME_TOK * blocks * 512 * WIDTH,
            bytes_accessed=blocks * 512 * WIDTH * 4,
            transcendentals=branches * FRAME_TOK * blocks * 512 * HERE,
        ),
    )(start, q, frames.reshape(-1, chunk), *(own or ()), *parts)


def log_sums(stats):
    s = stats[..., : 3 * HERE].astype(jnp.float32)
    return s.reshape(s.shape[:-1] + (HERE, 3)).sum(-1)


def out_kernel(a_ref, b_ref, wa_ref, wb_ref, o_ref):
    rows = a_ref.shape[1]
    for b in range(2):
        o_ref[b] = (
            jnp.dot(a_ref[b], wa_ref[...], preferred_element_type=jnp.float32)
            + jnp.dot(b_ref[b], wb_ref[...], preferred_element_type=jnp.float32)
        ).astype(jnp.bfloat16)


def project_out(a, b, wa, wb):
    rows, width, block = a.shape[1], wa.shape[1], 512
    return pl.pallas_call(
        out_kernel,
        grid=(width // block,),
        out_shape=jax.ShapeDtypeStruct((2, rows, width), jnp.bfloat16),
        in_specs=[
            pl.BlockSpec((2, rows, WIDTH), lambda i: (0, 0, 0)),
            pl.BlockSpec((2, rows, WIDTH), lambda i: (0, 0, 0)),
            pl.BlockSpec((WIDTH, block), lambda i: (0, i)),
            pl.BlockSpec((WIDTH, block), lambda i: (0, i)),
        ],
        out_specs=pl.BlockSpec((2, rows, block), lambda i: (0, 0, i)),
        compiler_params=pltpu.CompilerParams(vmem_limit_bytes=24 << 20),
        cost_estimate=pl.CostEstimate(
            flops=8 * rows * WIDTH * width,
            bytes_accessed=4 * WIDTH * width + 4 * rows * width,
            transcendentals=0,
        ),
    )(a, b, wa, wb)


def shards(x, actions, visible_from, table, w_qkv, w_out, ctx):
    branch = lax.axis_index("branch")
    core, base = branch % 2, branch // 8 * 8
    hidden, gate = norm(actions, x, jnp.transpose(table, (1, 0, 2)))
    w = jnp.transpose(w_qkv, (1, 0, 2))

    a0 = hidden
    a1, a3, b0 = along_seq(a0, 1), along_seq(a0, -1), along_seq(a0, 0, 1)
    a2 = jnp.concatenate([along_seq(a1[:1], 1), along_seq(a3[1:], -1)], axis=0)
    b1, b3 = along_seq(b0, 1), along_seq(b0, -1)
    b2 = along_seq(a2, 0, 1)

    ctx, _ = lax.optimization_barrier((ctx, hidden))
    mine = [ctx, along_branch(ctx, 1), along_branch(ctx, -1), along_branch(ctx, 2)]
    parts = mine + [along_branch(part, 0, 0, 1) for part in mine]
    at = branch // 2 % 4
    order = [base + (at + d) % 4 * 2 + c for c in (core, 1 - core) for d in (0, 3, 1, 2)]
    frames = jnp.stack(order)[:, None] * 2 + jnp.arange(512, dtype=jnp.int32) // FRAME_TOK
    far_start = along_branch(visible_from, 0, 1)

    half = w_out.shape[1] // 2
    near = across_z(lax.dynamic_slice_in_dim(w_out, core * half, half, 1))
    far = along_branch(near, 0, 0, 1)
    w_other = jnp.where(
        core == 0, jnp.concatenate([near, far], 1), jnp.concatenate([far, near], 1)
    )

    first = project_qkv([a0, a1, a3, b0], w)
    second = project_qkv([a2, b1, b3, b2], w)
    q, k, v = (
        jnp.concatenate([f[:, :96], s[:, :32], f[:, 96:], s[:, 32:]], axis=1)
        for f, s in zip(first, second)
    )
    far_q = along_branch(q, 0, 1)
    o_0, s_0 = attend(visible_from[:1], q[:1], frames, parts, (k[:1], v[:1]), jnp.float32)
    far_q, _ = lax.optimization_barrier((far_q, s_0))
    far_o = attend(far_start, far_q, frames, parts)
    packed = along_branch(jnp.concatenate(far_o, axis=2), 0, 1)
    o_1, s_1 = attend(visible_from[1:], q[1:], frames, parts, (k[1:], v[1:]), jnp.float32)
    own_o, own_l = jnp.concatenate([o_0, o_1]), log_sums(jnp.concatenate([s_0, s_1]))
    far_l = log_sums(packed[..., WIDTH:])
    top = jnp.maximum(own_l, far_l)
    own_w, far_w = jnp.exp2(own_l - top), jnp.exp2(far_l - top)
    total = own_w + far_w
    spread = lambda u: jnp.repeat(u / total, HDIM, axis=2)
    attended = (
        own_o * spread(own_w) + packed[..., :WIDTH].astype(jnp.float32) * spread(far_w)
    ).astype(jnp.bfloat16)

    here, there = attended[:, :128], attended[:, 128:]
    other = along_seq(there, 0, 1)
    p2 = project_out(here[:, 96:], other[:, 96:], w_out, w_other)
    down, up = along_seq(p2[:1], -1), along_seq(p2[1:], 1)
    rest = project_out(here[:, :96], other[:, :96], w_out, w_other).astype(jnp.float32)
    p0, p1, p3 = rest[:, :32], rest[:, 32:64], rest[:, 64:]
    p1 = jnp.concatenate([p1[:1] + down.astype(jnp.float32), p1[1:]]).astype(jnp.bfloat16)
    p3 = jnp.concatenate([p3[:1], p3[1:] + up.astype(jnp.float32)]).astype(jnp.bfloat16)
    t1, t3 = along_seq(p1, -1), along_seq(p3, 1)
    projected = p0 + t1.astype(jnp.float32) + t3.astype(jnp.float32)
    return (x.astype(jnp.float32) + gate * projected).astype(jnp.bfloat16)


def solution(mesh):
    in_specs = (
        P("branch", "seq", None),
        P("branch"),
        P("branch"),
        P(),
        P(None, None, "seq"),
        P("seq", None),
        P(None, "branch", "seq"),
    )
    out_specs = P("branch", "seq", None)
    return jax.shard_map(shards, mesh=mesh, in_specs=in_specs, out_specs=out_specs, check_vma=False)
```

```python
import functools
import math

import jax
import jax.numpy as jnp
from jax import lax
from jax.experimental import pallas as pl
from jax.experimental.pallas import tpu as pltpu
from jax.sharding import PartitionSpec as P

HDIM = 128
ACTIONS = 16
FRAME_TOK = 256
HERE = 3
WIDTH = HERE * HDIM
SCALE2 = math.log2(math.e) * HDIM ** (-0.5)
MASKED = -1e30
VMEM = pl.BlockSpec(memory_space=pltpu.VMEM)
SMEM = pl.BlockSpec(memory_space=pltpu.SMEM)
ANY = pl.BlockSpec(memory_space=pl.ANY)


def along_seq(a, dy=0, dz=0):
    perm = [
        (z * 4 + y, (z + dz) % 2 * 4 + (y + dy) % 4) for z in range(2) for y in range(4)
    ]
    return lax.ppermute(a, "seq", perm)


def along_branch(a, dx=0, dz=0, dc=0):
    perm = [
        ((z * 4 + x) * 2 + c, ((z + dz) % 2 * 4 + (x + dx) % 4) * 2 + (c + dc) % 2)
        for z in range(2)
        for x in range(4)
        for c in range(2)
    ]
    return lax.ppermute(a, "branch", perm)


def turned(a, axis, step):
    perm = []
    for b in range(16):
        for s in range(8):
            way = step if b % 2 == 0 else -step
            z, x, y = b // 8 * 8, b // 2 % 4, s % 4
            if axis == "x":
                to = (z + (x + way) % 4 * 2 + b % 2, s)
            else:
                to = (b, s - y + (y + way) % 4)
            perm.append((b * 8 + s, to[0] * 8 + to[1]))
    return lax.ppermute(a, ("branch", "seq"), perm)


def across_z(a):
    perm = []
    for b in range(16):
        for s in range(8):
            perm.append((b * 8 + s, (b + 8) % 16 * 8 + (s + 4) % 8))
    return lax.ppermute(a, ("branch", "seq"), perm)


def norm_kernel(actions, x_ref, table_ref, w_ref, hidden_ref, gate_ref, half_ref, sem):
    count = half_ref.shape[0]
    at = lax.rem(lax.axis_index("branch"), 2) * count
    copy = pltpu.make_async_copy(w_ref.at[pl.ds(pl.multiple_of(at, 16), count)], half_ref, sem)
    copy.start()
    rows = lax.broadcasted_iota(jnp.int32, (ACTIONS, 1), 0)
    for b in range(x_ref.shape[0]):
        pick = rows == actions[b]
        shift, scale, gate = (
            jnp.sum(
                jnp.where(pick, table_ref[c].astype(jnp.float32), 0.0), axis=0, keepdims=True
            )
            for c in range(3)
        )
        gate_ref[b] = gate
        x = x_ref[b].astype(jnp.float32)
        centred = x - jnp.mean(x, axis=-1, keepdims=True)
        variance = jnp.mean(centred * centred, axis=-1, keepdims=True)
        normed = centred * (1.0 / jnp.sqrt(variance + 1e-06))
        hidden_ref[b] = (normed * (1.0 + scale) + shift).astype(jnp.bfloat16)
    copy.wait()


def norm(actions, x, table, w_out):
    return pl.pallas_call(
        norm_kernel,
        out_shape=(
            jax.ShapeDtypeStruct(x.shape, jnp.bfloat16),
            jax.ShapeDtypeStruct((x.shape[0], 1, x.shape[2]), jnp.float32),
            jax.ShapeDtypeStruct((w_out.shape[0] // 2, w_out.shape[1]), w_out.dtype),
        ),
        in_specs=[SMEM, VMEM, VMEM, ANY],
        out_specs=(VMEM, VMEM, ANY),
        scratch_shapes=[pltpu.SemaphoreType.DMA],
        compiler_params=pltpu.CompilerParams(vmem_limit_bytes=24 << 20),
    )(actions, x, table, w_out)


def qkv_kernel(count, *refs):
    shards, w_ref, outs, acc = refs[:count], refs[count], refs[count + 1 : count + 4], refs[-1]
    step = pl.program_id(0)
    x = jnp.concatenate([s[b] for b in range(2) for s in shards], axis=0)

    @pl.when(step == 0)
    def _():
        acc[...] = jnp.zeros_like(acc)

    for c in range(3):
        acc[c] += jnp.dot(x, w_ref[c], preferred_element_type=jnp.float32)

    @pl.when(step == pl.num_programs(0) - 1)
    def _():
        rows = count * 32
        for c in range(3):
            for b in range(2):
                outs[c][b] = acc[c, b * rows : (b + 1) * rows].astype(jnp.bfloat16)


def project_qkv(shards, w):
    count, depth, block = len(shards), w.shape[1], 1024
    rows = count * 32
    out = jax.ShapeDtypeStruct((2, rows, WIDTH), jnp.bfloat16)
    return pl.pallas_call(
        functools.partial(qkv_kernel, count),
        grid=(depth // block,),
        out_shape=(out,) * 3,
        in_specs=[pl.BlockSpec((2, 32, block), lambda i: (0, 0, i))] * count
        + [pl.BlockSpec((3, block, WIDTH), lambda i: (0, i, 0))],
        out_specs=(pl.BlockSpec((2, rows, WIDTH), lambda i: (0, 0, 0)),) * 3,
        scratch_shapes=[pltpu.VMEM((3, 2 * rows, WIDTH), jnp.float32)],
        compiler_params=pltpu.CompilerParams(vmem_limit_bytes=32 << 20),
        cost_estimate=pl.CostEstimate(
            flops=2 * 2 * rows * depth * 3 * WIDTH,
            bytes_accessed=depth * 3 * WIDTH * 2 + 2 * rows * depth * 2,
            transcendentals=0,
        ),
    )(*shards, w)


def attend_kernel(branches, chunk, blocks, own, q_ref, frame_ref, *rest):
    if own:
        own_k, own_v, rest = rest[0], rest[1], rest[2:]
    parts, outs, (kv, top_s, sum_s, acc_s, sems) = rest[:blocks], rest[blocks:-5], rest[-5:]
    o_ref = outs[0]
    copies = [
        pltpu.make_async_copy(parts[i], kv.at[:, pl.ds(i * 512, 512)], sems.at[i])
        for i in range(blocks)
    ]
    for copy in copies:
        copy.start()

    def block_step(b, h, k, v, bias, first):
        q = q_ref[b, :FRAME_TOK, h * HDIM : (h + 1) * HDIM]
        s = lax.dot_general(q, k, (((1,), (1,)), ((), ())), preferred_element_type=jnp.float32)
        s = s * SCALE2
        if bias is not None:
            s = s + bias
        top = jnp.max(s, axis=1, keepdims=True)
        if first:
            new = jnp.broadcast_to(top, (FRAME_TOK, HDIM))
        else:
            old = top_s[b, h]
            new = jnp.maximum(old, top)
        p = jnp.exp2(s - new[:, :1])
        sums = p[:, :HDIM]
        for j in range(1, p.shape[1] // HDIM):
            sums = sums + p[:, j * HDIM : (j + 1) * HDIM]
        pv = jnp.dot(p.astype(jnp.bfloat16), v, preferred_element_type=jnp.float32)
        if first:
            sum_s[b, h] = sums
            acc_s[b, h] = pv
        else:
            factor = jnp.exp2(old - new)
            sum_s[b, h] = sum_s[b, h] * factor + sums
            acc_s[b, h] = acc_s[b, h] * factor + pv
        top_s[b, h] = new

    if own:
        for b in range(branches):
            for h in range(HERE):
                cols = slice(h * HDIM, (h + 1) * HDIM)
                block_step(b, h, own_k[b, :, cols], own_v[b, :, cols], None, True)
    else:
        top_s[...] = jnp.full_like(top_s[...], 2 * MASKED)
        sum_s[...] = jnp.zeros_like(sum_s[...])
        acc_s[...] = jnp.zeros_like(acc_s[...])
    for copy in copies:
        copy.wait()

    def loop(i, _):
        rows = pl.ds(pl.multiple_of(i * chunk, chunk), chunk)
        for b in range(branches):
            start = q_ref[b, FRAME_TOK:, :1].astype(jnp.float32)[:1]
            bias = jnp.where(frame_ref[pl.ds(i, 1), :] >= start, 0.0, MASKED)
            for h in range(HERE):
                cols = slice(h * HDIM, (h + 1) * HDIM)
                block_step(b, h, kv[0, rows, cols], kv[1, rows, cols], bias, False)
        return 0

    lax.fori_loop(0, blocks * 512 // chunk, loop, 0)
    lane = lax.broadcasted_iota(jnp.int32, (FRAME_TOK, HDIM), 1)
    for b in range(branches):
        stats = jnp.zeros((FRAME_TOK, HDIM), jnp.float32)
        for h in range(HERE):
            total = jnp.sum(sum_s[b, h], axis=1, keepdims=True)
            o_ref[b, :, h * HDIM : (h + 1) * HDIM] = (acc_s[b, h] / total).astype(o_ref.dtype)
            left = top_s[b, h] + jnp.log2(total)
            for part in range(3):
                piece = left.astype(jnp.bfloat16).astype(jnp.float32)
                stats = jnp.where(lane == h * 3 + part, piece, stats)
                left = left - piece
        if own:
            outs[1][b] = stats.astype(jnp.bfloat16)
        else:
            o_ref[b, :, WIDTH:] = stats.astype(jnp.bfloat16)


def attend(q, frames, parts, own=None):
    branches, blocks, chunk = q.shape[0], len(parts), 2048
    state = pltpu.VMEM((branches, HERE, FRAME_TOK, HDIM), jnp.float32)
    return pl.pallas_call(
        functools.partial(attend_kernel, branches, chunk, blocks, own is not None),
        out_shape=(
            jax.ShapeDtypeStruct((branches, FRAME_TOK, WIDTH), jnp.float32),
            jax.ShapeDtypeStruct((branches, FRAME_TOK, HDIM), jnp.bfloat16),
        )
        if own
        else jax.ShapeDtypeStruct((branches, FRAME_TOK, WIDTH + HDIM), jnp.bfloat16),
        in_specs=[VMEM, VMEM] + ([VMEM, VMEM] if own else []) + [ANY] * blocks,
        out_specs=(VMEM, VMEM) if own else VMEM,
        scratch_shapes=[
            pltpu.VMEM((2, blocks * 512, WIDTH), jnp.bfloat16),
            state,
            state,
            state,
            pltpu.SemaphoreType.DMA((blocks,)),
        ],
        compiler_params=pltpu.CompilerParams(vmem_limit_bytes=40 << 20),
        cost_estimate=pl.CostEstimate(
            flops=8 * branches * FRAME_TOK * blocks * 512 * WIDTH,
            bytes_accessed=blocks * 512 * WIDTH * 4,
            transcendentals=branches * FRAME_TOK * blocks * 512 * HERE,
        ),
    )(q, frames.reshape(-1, chunk), *(own or ()), *parts)


def merge_kernel(*refs):
    here, there = refs[-2:]
    packed = refs[-3]
    count = (len(refs) - 3) // 2
    for b in range(count):
        o_ref, stat_ref = refs[2 * b : 2 * b + 2]
        for h in range(HERE):
            cols = slice(h * HDIM, (h + 1) * HDIM)
            own = stat_ref[0, :, h * 3 : h * 3 + 3].astype(jnp.float32)
            far = packed[b, :, WIDTH + h * 3 : WIDTH + h * 3 + 3].astype(jnp.float32)
            own = jnp.sum(own, axis=1, keepdims=True)
            far = jnp.sum(far, axis=1, keepdims=True)
            top = jnp.maximum(own, far)
            own, far = jnp.exp2(own - top), jnp.exp2(far - top)
            scale = 1.0 / (own + far)
            o = (
                o_ref[0, :, cols] * (own * scale)
                + packed[b, :, cols].astype(jnp.float32) * (far * scale)
            ).astype(jnp.bfloat16)
            here[b, :, cols] = o[:128]
            there[b, :, cols] = o[128:]


def merge(parts, packed):
    out = jax.ShapeDtypeStruct((len(parts), 128, WIDTH), jnp.bfloat16)
    flat = [a for part in parts for a in part]
    return pl.pallas_call(
        merge_kernel,
        out_shape=(out, out),
        in_specs=[VMEM] * (len(flat) + 1),
        out_specs=(VMEM, VMEM),
        compiler_params=pltpu.CompilerParams(vmem_limit_bytes=24 << 20),
    )(*flat, packed)


def out_kernel(core, a_ref, b_ref, wa_ref, near_ref, far_ref, *rest):
    outs, w = rest[:-1], rest[-1]
    half = near_ref.shape[0]
    for side, ref in ((core[0], near_ref), (1 - core[0], far_ref)):
        w[pl.ds(pl.multiple_of(side * half, 16), half)] = ref[...]
    rows = a_ref.shape[1]
    stack = lambda ref: jnp.concatenate([ref[b] for b in range(ref.shape[0])], axis=0)
    o = (
        jnp.dot(stack(a_ref), wa_ref[...], preferred_element_type=jnp.float32)
        + jnp.dot(stack(b_ref), w[...], preferred_element_type=jnp.float32)
    ).astype(jnp.bfloat16)
    for b in range(a_ref.shape[0]):
        for j, ref in enumerate(outs):
            ref[b] = o[b * rows + j * 32 : b * rows + (j + 1) * 32]


def project_out(core, a, b, wa, near, far):
    branches, rows, width, block = a.shape[0], a.shape[1], wa.shape[1], 512
    count = rows // 32
    return pl.pallas_call(
        out_kernel,
        grid=(width // block,),
        out_shape=(jax.ShapeDtypeStruct((branches, 32, width), jnp.bfloat16),) * count,
        in_specs=[
            SMEM,
            pl.BlockSpec((branches, rows, WIDTH), lambda i: (0, 0, 0)),
            pl.BlockSpec((branches, rows, WIDTH), lambda i: (0, 0, 0)),
            pl.BlockSpec((WIDTH, block), lambda i: (0, i)),
        ]
        + [pl.BlockSpec((WIDTH // 2, block), lambda i: (0, i))] * 2,
        out_specs=(pl.BlockSpec((branches, 32, block), lambda i: (0, 0, i)),) * count,
        scratch_shapes=[pltpu.VMEM((WIDTH, block), jnp.bfloat16)],
        compiler_params=pltpu.CompilerParams(vmem_limit_bytes=24 << 20),
        cost_estimate=pl.CostEstimate(
            flops=4 * branches * rows * WIDTH * width,
            bytes_accessed=4 * WIDTH * width + 2 * branches * rows * width,
            transcendentals=0,
        ),
    )(core, a, b, wa, near, far)


def shards(x, actions, visible_from, table, w_qkv, w_out, ctx):
    branch = lax.axis_index("branch")
    core, base = branch % 2, branch // 8 * 8
    hidden, gate, half = norm(actions, x, jnp.transpose(table, (1, 0, 2)), w_out)
    w = jnp.transpose(w_qkv, (1, 0, 2))

    a0 = hidden
    a1, a3, b0 = turned(a0, "y", 1), turned(a0, "y", -1), along_seq(a0, 0, 1)
    a2 = turned(a1, "y", 1)
    b1, b3 = turned(b0, "y", 1), turned(b0, "y", -1)
    b2 = along_seq(a2, 0, 1)

    near = across_z(half)
    far = along_branch(near, 0, 0, 1)

    ctx, _ = lax.optimization_barrier((ctx, hidden))
    c1 = turned(ctx, "x", 1)
    c3 = turned(lax.optimization_barrier((ctx, c1))[0], "x", -1)
    c2 = turned(lax.optimization_barrier((c1, c3))[0], "x", 1)
    mine = [ctx, c1, c3, c2]
    parts = mine + [along_branch(part, 0, 0, 1) for part in mine]
    at = branch // 2 % 4
    order = []
    for c in (core, 1 - core):
        for d in (0, 2 * c - 1, 1 - 2 * c, 2):
            order.append(base + (at + d + 4) % 4 * 2 + c)
    frames = jnp.stack(order)[:, None] * 2 + jnp.arange(512, dtype=jnp.int32) // FRAME_TOK
    frames = frames.astype(jnp.float32)

    first = project_qkv([a0, a1, a3, b0], w)
    second = project_qkv([a2, b1, b3, b2], w)
    start = jnp.broadcast_to(visible_from.astype(jnp.bfloat16)[:, None, None], (2, 16, WIDTH))
    q, k, v = (
        jnp.concatenate([f[:, :96], s[:, :32], f[:, 96:], s[:, 32:]] + tail, axis=1)
        for f, s, tail in zip(first, second, ([start], [], []))
    )
    far_q = along_branch(q, 0, 1)
    o_0, s_0 = attend(q[:1], frames, parts, (k[:1], v[:1]))
    far_q, _ = lax.optimization_barrier((far_q, s_0))
    packed = along_branch(attend(far_q, frames, parts), 0, 1)
    o_1, s_1 = attend(q[1:], frames, parts, (k[1:], v[1:]))
    here, there = merge([(o_0, s_0), (o_1, s_1)], packed)
    other = along_seq(there, 0, 1)
    p0, p1, p3, p2 = project_out(
        core.astype(jnp.int32).reshape(1), here, other, w_out, near, far
    )
    back = turned(p2, "y", -1)
    t3 = turned(p3, "y", 1)
    p1 = (p1.astype(jnp.float32) + back.astype(jnp.float32)).astype(jnp.bfloat16)
    t1 = turned(p1, "y", -1)
    sums = p0.astype(jnp.float32) + t1.astype(jnp.float32) + t3.astype(jnp.float32)
    return (x.astype(jnp.float32) + gate * sums).astype(jnp.bfloat16)


def solution(mesh):
    in_specs = (
        P("branch", "seq", None),
        P("branch"),
        P("branch"),
        P(),
        P(None, None, "seq"),
        P("seq", None),
        P(None, "branch", "seq"),
    )
    out_specs = P("branch", "seq", None)
    return jax.shard_map(shards, mesh=mesh, in_specs=in_specs, out_specs=out_specs, check_vma=False)
```

```python
import functools
import math

import jax
import jax.numpy as jnp
from jax import lax
from jax.experimental import pallas as pl
from jax.experimental.pallas import tpu as pltpu
from jax.sharding import PartitionSpec as P

HDIM = 128
ACTIONS = 16
FRAME_TOK = 256
HERE = 3
WIDTH = HERE * HDIM
SCALE2 = math.log2(math.e) * HDIM ** (-0.5)
MASKED = -1e30
VMEM = pl.BlockSpec(memory_space=pltpu.VMEM)
SMEM = pl.BlockSpec(memory_space=pltpu.SMEM)
ANY = pl.BlockSpec(memory_space=pl.ANY)


def along_seq(a, dy=0, dz=0):
    perm = [
        (z * 4 + y, (z + dz) % 2 * 4 + (y + dy) % 4) for z in range(2) for y in range(4)
    ]
    return lax.ppermute(a, "seq", perm)


def along_branch(a, dx=0, dz=0, dc=0):
    perm = [
        ((z * 4 + x) * 2 + c, ((z + dz) % 2 * 4 + (x + dx) % 4) * 2 + (c + dc) % 2)
        for z in range(2)
        for x in range(4)
        for c in range(2)
    ]
    return lax.ppermute(a, "branch", perm)


def turned(a, axis, step):
    perm = []
    for b in range(16):
        for s in range(8):
            way = step if b % 2 == 0 else -step
            z, x, y = b // 8 * 8, b // 2 % 4, s % 4
            if axis == "x":
                to = (z + (x + way) % 4 * 2 + b % 2, s)
            else:
                to = (b, s - y + (y + way) % 4)
            perm.append((b * 8 + s, to[0] * 8 + to[1]))
    return lax.ppermute(a, ("branch", "seq"), perm)


def across_z(a):
    perm = []
    for b in range(16):
        for s in range(8):
            perm.append((b * 8 + s, (b + 8) % 16 * 8 + (s + 4) % 8))
    return lax.ppermute(a, ("branch", "seq"), perm)


def norm_kernel(
    actions, x_hbm, table_hbm, w_hbm, hidden_ref, gate_ref, w_0, w_1, x_ref, table_ref, sems
):
    count = w_0.shape[0]
    at = lax.rem(lax.axis_index("branch"), 2) * 2 * count
    quarters = [pl.ds(pl.multiple_of(at + j * count, 16), count) for j in range(2)]
    copies = [
        pltpu.make_async_copy(x_hbm, x_ref, sems.at[0]),
        pltpu.make_async_copy(table_hbm, table_ref, sems.at[1]),
        pltpu.make_async_copy(w_hbm.at[quarters[0]], w_0, sems.at[2]),
        pltpu.make_async_copy(w_hbm.at[quarters[1]], w_1, sems.at[3]),
    ]
    for copy in copies:
        copy.start()
    copies[0].wait()
    copies[1].wait()
    rows = lax.broadcasted_iota(jnp.int32, (ACTIONS, 1), 0)
    for b in range(x_ref.shape[0]):
        pick = rows == actions[b]
        shift, scale, gate = (
            jnp.sum(
                jnp.where(pick, table_ref[c].astype(jnp.float32), 0.0), axis=0, keepdims=True
            )
            for c in range(3)
        )
        gate_ref[b] = gate
        x = x_ref[b].astype(jnp.float32)
        centred = x - jnp.mean(x, axis=-1, keepdims=True)
        variance = jnp.mean(centred * centred, axis=-1, keepdims=True)
        normed = centred * (1.0 / jnp.sqrt(variance + 1e-06))
        hidden_ref[b] = (normed * (1.0 + scale) + shift).astype(jnp.bfloat16)
    copies[2].wait()
    copies[3].wait()


def norm(actions, x, table, w_out):
    quarter = jax.ShapeDtypeStruct((w_out.shape[0] // 4, w_out.shape[1]), w_out.dtype)
    return pl.pallas_call(
        norm_kernel,
        out_shape=(
            jax.ShapeDtypeStruct(x.shape, jnp.bfloat16),
            jax.ShapeDtypeStruct((x.shape[0], 1, x.shape[2]), jnp.float32),
            quarter,
            quarter,
        ),
        in_specs=[SMEM, ANY, ANY, ANY],
        out_specs=(VMEM,) * 4,
        scratch_shapes=[
            pltpu.VMEM(x.shape, x.dtype),
            pltpu.VMEM(table.shape, table.dtype),
            pltpu.SemaphoreType.DMA((4,)),
        ],
        compiler_params=pltpu.CompilerParams(vmem_limit_bytes=56 << 20),
    )(actions, x, table, w_out)


def qkv_kernel(count, *refs):
    shards, w_ref, outs, acc = refs[:count], refs[count], refs[count + 1 : count + 4], refs[-1]
    step = pl.program_id(0)
    x = jnp.concatenate([s[b] for b in range(2) for s in shards], axis=0)

    @pl.when(step == 0)
    def _():
        acc[...] = jnp.zeros_like(acc)

    for c in range(3):
        acc[c] += jnp.dot(x, w_ref[c], preferred_element_type=jnp.float32)

    @pl.when(step == pl.num_programs(0) - 1)
    def _():
        rows = count * 32
        for c in range(3):
            for b in range(2):
                outs[c][b] = acc[c, b * rows : (b + 1) * rows].astype(jnp.bfloat16)


def project_qkv(shards, w):
    count, depth, block = len(shards), w.shape[1], 1024
    rows = count * 32
    out = jax.ShapeDtypeStruct((2, rows, WIDTH), jnp.bfloat16)
    return pl.pallas_call(
        functools.partial(qkv_kernel, count),
        grid=(depth // block,),
        out_shape=(out,) * 3,
        in_specs=[pl.BlockSpec((2, 32, block), lambda i: (0, 0, i))] * count
        + [pl.BlockSpec((3, block, WIDTH), lambda i: (0, i, 0))],
        out_specs=(pl.BlockSpec((2, rows, WIDTH), lambda i: (0, 0, 0)),) * 3,
        scratch_shapes=[pltpu.VMEM((3, 2 * rows, WIDTH), jnp.float32)],
        compiler_params=pltpu.CompilerParams(vmem_limit_bytes=32 << 20),
        cost_estimate=pl.CostEstimate(
            flops=2 * 2 * rows * depth * 3 * WIDTH,
            bytes_accessed=depth * 3 * WIDTH * 2 + 2 * rows * depth * 2,
            transcendentals=0,
        ),
    )(*shards, w)


def attend_kernel(branches, chunk, blocks, own, q_ref, frame_ref, *rest):
    if own:
        own_k, own_v, rest = rest[0], rest[1], rest[2:]
    parts, outs, (kv, top_s, sum_s, acc_s, sems) = rest[:blocks], rest[blocks:-5], rest[-5:]
    o_ref = outs[0]
    copies = [
        pltpu.make_async_copy(parts[i], kv.at[:, pl.ds(i * 512, 512)], sems.at[i])
        for i in range(blocks)
    ]
    for copy in copies:
        copy.start()

    def block_step(b, h, k, v, bias, first):
        q = q_ref[b, :FRAME_TOK, h * HDIM : (h + 1) * HDIM]
        s = lax.dot_general(q, k, (((1,), (1,)), ((), ())), preferred_element_type=jnp.float32)
        s = s * SCALE2
        if bias is not None:
            s = s + bias
        top = jnp.max(s, axis=1, keepdims=True)
        if first:
            new = jnp.broadcast_to(top, (FRAME_TOK, HDIM))
        else:
            old = top_s[b, h]
            new = jnp.maximum(old, top)
        p = jnp.exp2(s - new[:, :1])
        sums = p[:, :HDIM]
        for j in range(1, p.shape[1] // HDIM):
            sums = sums + p[:, j * HDIM : (j + 1) * HDIM]
        pv = jnp.dot(p.astype(jnp.bfloat16), v, preferred_element_type=jnp.float32)
        if first:
            sum_s[b, h] = sums
            acc_s[b, h] = pv
        else:
            factor = jnp.exp2(old - new)
            sum_s[b, h] = sum_s[b, h] * factor + sums
            acc_s[b, h] = acc_s[b, h] * factor + pv
        top_s[b, h] = new

    if own:
        for b in range(branches):
            for h in range(HERE):
                cols = slice(h * HDIM, (h + 1) * HDIM)
                block_step(b, h, own_k[b, :, cols], own_v[b, :, cols], None, True)
    else:
        top_s[...] = jnp.full_like(top_s[...], 2 * MASKED)
        sum_s[...] = jnp.zeros_like(sum_s[...])
        acc_s[...] = jnp.zeros_like(acc_s[...])
    for copy in copies:
        copy.wait()

    def loop(i, _):
        rows = pl.ds(pl.multiple_of(i * chunk, chunk), chunk)
        for b in range(branches):
            start = q_ref[b, FRAME_TOK:, :1].astype(jnp.float32)[:1]
            bias = jnp.where(frame_ref[pl.ds(i, 1), :] >= start, 0.0, MASKED)
            for h in range(HERE):
                cols = slice(h * HDIM, (h + 1) * HDIM)
                block_step(b, h, kv[0, rows, cols], kv[1, rows, cols], bias, False)
        return 0

    lax.fori_loop(0, blocks * 512 // chunk, loop, 0)
    lane = lax.broadcasted_iota(jnp.int32, (FRAME_TOK, HDIM), 1)
    for b in range(branches):
        stats = jnp.zeros((FRAME_TOK, HDIM), jnp.float32)
        for h in range(HERE):
            total = jnp.sum(sum_s[b, h], axis=1, keepdims=True)
            o_ref[b, :, h * HDIM : (h + 1) * HDIM] = (acc_s[b, h] / total).astype(o_ref.dtype)
            left = top_s[b, h] + jnp.log2(total)
            for part in range(3):
                piece = left.astype(jnp.bfloat16).astype(jnp.float32)
                stats = jnp.where(lane == h * 3 + part, piece, stats)
                left = left - piece
        if own:
            outs[1][b] = stats.astype(jnp.bfloat16)
        else:
            o_ref[b, :, WIDTH:] = stats.astype(jnp.bfloat16)


def attend(q, frames, parts, own=None):
    branches, blocks, chunk = q.shape[0], len(parts), 2048
    state = pltpu.VMEM((branches, HERE, FRAME_TOK, HDIM), jnp.float32)
    return pl.pallas_call(
        functools.partial(attend_kernel, branches, chunk, blocks, own is not None),
        out_shape=(
            jax.ShapeDtypeStruct((branches, FRAME_TOK, WIDTH), jnp.float32),
            jax.ShapeDtypeStruct((branches, FRAME_TOK, HDIM), jnp.bfloat16),
        )
        if own
        else jax.ShapeDtypeStruct((branches, FRAME_TOK, WIDTH + HDIM), jnp.bfloat16),
        in_specs=[VMEM, VMEM] + ([VMEM, VMEM] if own else []) + [ANY] * blocks,
        out_specs=(VMEM, VMEM) if own else VMEM,
        scratch_shapes=[
            pltpu.VMEM((2, blocks * 512, WIDTH), jnp.bfloat16),
            state,
            state,
            state,
            pltpu.SemaphoreType.DMA((blocks,)),
        ],
        compiler_params=pltpu.CompilerParams(vmem_limit_bytes=40 << 20),
        cost_estimate=pl.CostEstimate(
            flops=8 * branches * FRAME_TOK * blocks * 512 * WIDTH,
            bytes_accessed=blocks * 512 * WIDTH * 4,
            transcendentals=branches * FRAME_TOK * blocks * 512 * HERE,
        ),
    )(q, frames.reshape(-1, chunk), *(own or ()), *parts)


def merge_kernel(*refs):
    here, there = refs[-2:]
    packed = refs[-3]
    count = (len(refs) - 3) // 2
    for b in range(count):
        o_ref, stat_ref = refs[2 * b : 2 * b + 2]
        for h in range(HERE):
            cols = slice(h * HDIM, (h + 1) * HDIM)
            own = stat_ref[0, :, h * 3 : h * 3 + 3].astype(jnp.float32)
            far = packed[b, :, WIDTH + h * 3 : WIDTH + h * 3 + 3].astype(jnp.float32)
            own = jnp.sum(own, axis=1, keepdims=True)
            far = jnp.sum(far, axis=1, keepdims=True)
            top = jnp.maximum(own, far)
            own, far = jnp.exp2(own - top), jnp.exp2(far - top)
            scale = 1.0 / (own + far)
            o = (
                o_ref[0, :, cols] * (own * scale)
                + packed[b, :, cols].astype(jnp.float32) * (far * scale)
            ).astype(jnp.bfloat16)
            here[b, :, cols] = o[:128]
            there[b, :, cols] = o[128:]


def merge(parts, packed):
    out = jax.ShapeDtypeStruct((len(parts), 128, WIDTH), jnp.bfloat16)
    flat = [a for part in parts for a in part]
    return pl.pallas_call(
        merge_kernel,
        out_shape=(out, out),
        in_specs=[VMEM] * (len(flat) + 1),
        out_specs=(VMEM, VMEM),
        compiler_params=pltpu.CompilerParams(vmem_limit_bytes=24 << 20),
    )(*flat, packed)


def out_kernel(core, a_ref, b_ref, wa_ref, *rest):
    pieces, outs, w = rest[:4], rest[4:-1], rest[-1]
    count, depth = pieces[0].shape[0], wa_ref.shape[0]
    w[:depth] = wa_ref[...]
    for j, ref in enumerate(pieces):
        side = core[0] if j < 2 else 1 - core[0]
        at = depth + (side * 2 + j % 2) * count
        w[pl.ds(pl.multiple_of(at, 16), count)] = ref[...]
    rows, branches = a_ref.shape[1], range(a_ref.shape[0])
    x = jnp.concatenate(
        [jnp.concatenate([ref[b] for b in branches], axis=0) for ref in (a_ref, b_ref)], axis=1
    )
    o = jnp.dot(x, w[...], preferred_element_type=jnp.float32).astype(jnp.bfloat16)
    for b in range(a_ref.shape[0]):
        for j, ref in enumerate(outs):
            ref[b] = o[b * rows + j * 32 : b * rows + (j + 1) * 32]


def project_out(core, a, b, wa, pieces):
    branches, rows, width, block = a.shape[0], a.shape[1], wa.shape[1], 512
    count = rows // 32
    return pl.pallas_call(
        out_kernel,
        grid=(width // block,),
        out_shape=(jax.ShapeDtypeStruct((branches, 32, width), jnp.bfloat16),) * count,
        in_specs=[
            SMEM,
            pl.BlockSpec((branches, rows, WIDTH), lambda i: (0, 0, 0)),
            pl.BlockSpec((branches, rows, WIDTH), lambda i: (0, 0, 0)),
            pl.BlockSpec((WIDTH, block), lambda i: (0, i)),
        ]
        + [pl.BlockSpec((WIDTH // 4, block), lambda i: (0, i))] * 4,
        out_specs=(pl.BlockSpec((branches, 32, block), lambda i: (0, 0, i)),) * count,
        scratch_shapes=[pltpu.VMEM((2 * WIDTH, block), jnp.bfloat16)],
        compiler_params=pltpu.CompilerParams(vmem_limit_bytes=24 << 20),
        cost_estimate=pl.CostEstimate(
            flops=4 * branches * rows * WIDTH * width,
            bytes_accessed=4 * WIDTH * width + 2 * branches * rows * width,
            transcendentals=0,
        ),
    )(core, a, b, wa, *pieces)


def shards(x, actions, visible_from, table, w_qkv, w_out, ctx):
    branch = lax.axis_index("branch")
    core, base = branch % 2, branch // 8 * 8
    hidden, gate, *quarters = norm(actions, x, jnp.transpose(table, (1, 0, 2)), w_out)
    w = jnp.transpose(w_qkv, (1, 0, 2))

    a0 = hidden
    a1, a3, b0 = turned(a0, "y", 1), turned(a0, "y", -1), along_seq(a0, 0, 1)
    a2 = turned(a1, "y", 1)
    b1, b3 = turned(b0, "y", 1), turned(b0, "y", -1)
    b2 = along_seq(a2, 0, 1)

    near = across_z(quarters[0])
    b2, near = lax.optimization_barrier((b2, near))
    far = along_branch(near, 0, 0, 1)

    ctx, _ = lax.optimization_barrier((ctx, hidden))
    c1 = turned(ctx, "x", 1)
    c3 = turned(ctx, "x", -1)
    c2 = turned(c1, "x", 1)
    mine = [ctx, c1, c3, c2]
    parts = list(mine)
    for part in mine:
        part, _ = lax.optimization_barrier((part, b0))
        parts.append(along_branch(part, 0, 0, 1))
    at = branch // 2 % 4
    order = []
    for c in (core, 1 - core):
        for d in (0, 2 * c - 1, 1 - 2 * c, 2):
            order.append(base + (at + d + 4) % 4 * 2 + c)
    frames = jnp.stack(order)[:, None] * 2 + jnp.arange(512, dtype=jnp.int32) // FRAME_TOK
    frames = frames.astype(jnp.float32)

    first = project_qkv([a0, a1, a3, b0], w)
    second = project_qkv([a2, b1, b3, b2], w)
    start = jnp.broadcast_to(visible_from.astype(jnp.bfloat16)[:, None, None], (2, 16, WIDTH))
    q, k, v = (
        jnp.concatenate([f[:, :96], s[:, :32], f[:, 96:], s[:, 32:]] + tail, axis=1)
        for f, s, tail in zip(first, second, ([start], [], []))
    )
    far_q = along_branch(q, 0, 1)
    quarter, _ = lax.optimization_barrier((quarters[1], q))
    near_1 = across_z(quarter)
    o_0, s_0 = attend(q[:1], frames, parts, (k[:1], v[:1]))
    far_q, _ = lax.optimization_barrier((far_q, s_0))
    far_o = attend(far_q, frames, parts)
    packed = along_branch(far_o, 0, 1)
    last, _ = lax.optimization_barrier((q[1:], far_o))
    o_1, s_1 = attend(last, frames, parts, (k[1:], v[1:]))
    near_1, packed, o_1 = lax.optimization_barrier((near_1, packed, o_1))
    pieces = [near, near_1, far, along_branch(near_1, 0, 0, 1)]
    here, there = merge([(o_0, s_0), (o_1, s_1)], packed)
    other = along_seq(there, 0, 1)
    p0, p1, p3, p2 = project_out(
        core.astype(jnp.int32).reshape(1), here, other, w_out, pieces
    )
    back = turned(p2, "y", -1)
    t3 = turned(p3, "y", 1)
    p1 = (p1.astype(jnp.float32) + back.astype(jnp.float32)).astype(jnp.bfloat16)
    t1 = turned(p1, "y", -1)
    sums = p0.astype(jnp.float32) + t1.astype(jnp.float32) + t3.astype(jnp.float32)
    return (x.astype(jnp.float32) + gate * sums).astype(jnp.bfloat16)


def solution(mesh):
    in_specs = (
        P("branch", "seq", None),
        P("branch"),
        P("branch"),
        P(),
        P(None, None, "seq"),
        P("seq", None),
        P(None, "branch", "seq"),
    )
    out_specs = P("branch", "seq", None)
    return jax.shard_map(shards, mesh=mesh, in_specs=in_specs, out_specs=out_specs, check_vma=False)
```

```python
import functools
import math

import jax
import jax.numpy as jnp
from jax import lax
from jax.experimental import pallas as pl
from jax.experimental.pallas import tpu as pltpu
from jax.sharding import PartitionSpec as P

HDIM = 128
ACTIONS = 16
FRAME_TOK = 256
HERE = 3
WIDTH = HERE * HDIM
SCALE2 = math.log2(math.e) * HDIM ** (-0.5)
MASKED = -1e30
VMEM = pl.BlockSpec(memory_space=pltpu.VMEM)
SMEM = pl.BlockSpec(memory_space=pltpu.SMEM)
ANY = pl.BlockSpec(memory_space=pl.ANY)


def along_seq(a, dy=0, dz=0):
    perm = [
        (z * 4 + y, (z + dz) % 2 * 4 + (y + dy) % 4) for z in range(2) for y in range(4)
    ]
    return lax.ppermute(a, "seq", perm)


def along_branch(a, dx=0, dz=0, dc=0):
    perm = [
        ((z * 4 + x) * 2 + c, ((z + dz) % 2 * 4 + (x + dx) % 4) * 2 + (c + dc) % 2)
        for z in range(2)
        for x in range(4)
        for c in range(2)
    ]
    return lax.ppermute(a, "branch", perm)


def turned(a, axis, step):
    perm = []
    for b in range(16):
        for s in range(8):
            way = step if b % 2 == 0 else -step
            z, x, y = b // 8 * 8, b // 2 % 4, s % 4
            if axis == "x":
                to = (z + (x + way) % 4 * 2 + b % 2, s)
            else:
                to = (b, s - y + (y + way) % 4)
            perm.append((b * 8 + s, to[0] * 8 + to[1]))
    return lax.ppermute(a, ("branch", "seq"), perm)


def across_z(a):
    perm = []
    for b in range(16):
        for s in range(8):
            perm.append((b * 8 + s, (b + 8) % 16 * 8 + (s + 4) % 8))
    return lax.ppermute(a, ("branch", "seq"), perm)


def norm_kernel(
    actions, x_hbm, table_hbm, w_hbm, hidden_ref, gate_ref, w_0, w_1, x_ref, table_ref, sems
):
    count = w_0.shape[0]
    at = lax.rem(lax.axis_index("branch"), 2) * 2 * count
    quarters = [pl.ds(pl.multiple_of(at + j * count, 16), count) for j in range(2)]
    copies = [
        pltpu.make_async_copy(x_hbm, x_ref, sems.at[0]),
        pltpu.make_async_copy(table_hbm, table_ref, sems.at[1]),
        pltpu.make_async_copy(w_hbm.at[quarters[0]], w_0, sems.at[2]),
        pltpu.make_async_copy(w_hbm.at[quarters[1]], w_1, sems.at[3]),
    ]
    for copy in copies:
        copy.start()
    copies[0].wait()
    copies[1].wait()
    rows = lax.broadcasted_iota(jnp.int32, (ACTIONS, 1), 0)
    for b in range(x_ref.shape[0]):
        pick = rows == actions[b]
        shift, scale, gate = (
            jnp.sum(
                jnp.where(pick, table_ref[c].astype(jnp.float32), 0.0), axis=0, keepdims=True
            )
            for c in range(3)
        )
        gate_ref[b] = gate
        x = x_ref[b].astype(jnp.float32)
        centred = x - jnp.mean(x, axis=-1, keepdims=True)
        variance = jnp.mean(centred * centred, axis=-1, keepdims=True)
        normed = centred * (1.0 / jnp.sqrt(variance + 1e-06))
        hidden_ref[b] = (normed * (1.0 + scale) + shift).astype(jnp.bfloat16)
    copies[2].wait()
    copies[3].wait()


def norm(actions, x, table, w_out):
    quarter = jax.ShapeDtypeStruct((w_out.shape[0] // 4, w_out.shape[1]), w_out.dtype)
    return pl.pallas_call(
        norm_kernel,
        out_shape=(
            jax.ShapeDtypeStruct(x.shape, jnp.bfloat16),
            jax.ShapeDtypeStruct((x.shape[0], 1, x.shape[2]), jnp.float32),
            quarter,
            quarter,
        ),
        in_specs=[SMEM, ANY, ANY, ANY],
        out_specs=(VMEM,) * 4,
        scratch_shapes=[
            pltpu.VMEM(x.shape, x.dtype),
            pltpu.VMEM(table.shape, table.dtype),
            pltpu.SemaphoreType.DMA((4,)),
        ],
        compiler_params=pltpu.CompilerParams(vmem_limit_bytes=56 << 20),
    )(actions, x, table, w_out)


def qkv_kernel(count, *refs):
    shards, w_ref, outs, acc = refs[:count], refs[count], refs[count + 1 : count + 4], refs[-1]
    step = pl.program_id(0)
    x = jnp.concatenate([s[b] for b in range(2) for s in shards], axis=0)

    @pl.when(step == 0)
    def _():
        acc[...] = jnp.zeros_like(acc)

    for c in range(3):
        acc[c] += jnp.dot(x, w_ref[c], preferred_element_type=jnp.float32)

    @pl.when(step == pl.num_programs(0) - 1)
    def _():
        rows = count * 32
        for c in range(3):
            for b in range(2):
                outs[c][b] = acc[c, b * rows : (b + 1) * rows].astype(jnp.bfloat16)


def project_qkv(shards, w):
    count, depth, block = len(shards), w.shape[1], 1024
    rows = count * 32
    out = jax.ShapeDtypeStruct((2, rows, WIDTH), jnp.bfloat16)
    return pl.pallas_call(
        functools.partial(qkv_kernel, count),
        grid=(depth // block,),
        out_shape=(out,) * 3,
        in_specs=[pl.BlockSpec((2, 32, block), lambda i: (0, 0, i))] * count
        + [pl.BlockSpec((3, block, WIDTH), lambda i: (0, i, 0))],
        out_specs=(pl.BlockSpec((2, rows, WIDTH), lambda i: (0, 0, 0)),) * 3,
        scratch_shapes=[pltpu.VMEM((3, 2 * rows, WIDTH), jnp.float32)],
        compiler_params=pltpu.CompilerParams(vmem_limit_bytes=32 << 20),
        cost_estimate=pl.CostEstimate(
            flops=2 * 2 * rows * depth * 3 * WIDTH,
            bytes_accessed=depth * 3 * WIDTH * 2 + 2 * rows * depth * 2,
            transcendentals=0,
        ),
    )(*shards, w)


def attend_kernel(branches, chunk, blocks, own, q_ref, frame_ref, *rest):
    if own:
        own_k, own_v, rest = rest[0], rest[1], rest[2:]
    parts, outs, (kv, top_s, sum_s, acc_s, sems) = rest[:blocks], rest[blocks:-5], rest[-5:]
    o_ref = outs[0]
    copies = [
        pltpu.make_async_copy(parts[i], kv.at[:, pl.ds(i * 512, 512)], sems.at[i])
        for i in range(blocks)
    ]
    for copy in copies:
        copy.start()

    def block_step(b, h, k, v, bias, first):
        q = q_ref[b, :FRAME_TOK, h * HDIM : (h + 1) * HDIM]
        s = lax.dot_general(q, k, (((1,), (1,)), ((), ())), preferred_element_type=jnp.float32)
        s = s * SCALE2
        if bias is not None:
            s = s + bias
        top = jnp.max(s, axis=1, keepdims=True)
        if first:
            new = jnp.broadcast_to(top, (FRAME_TOK, HDIM))
        else:
            old = top_s[b, h]
            new = jnp.maximum(old, top)
        p = jnp.exp2(s - new[:, :1])
        sums = p[:, :HDIM]
        for j in range(1, p.shape[1] // HDIM):
            sums = sums + p[:, j * HDIM : (j + 1) * HDIM]
        pv = jnp.dot(p.astype(jnp.bfloat16), v, preferred_element_type=jnp.float32)
        if first:
            sum_s[b, h] = sums
            acc_s[b, h] = pv
        else:
            factor = jnp.exp2(old - new)
            sum_s[b, h] = sum_s[b, h] * factor + sums
            acc_s[b, h] = acc_s[b, h] * factor + pv
        top_s[b, h] = new

    if own:
        for b in range(branches):
            for h in range(HERE):
                cols = slice(h * HDIM, (h + 1) * HDIM)
                block_step(b, h, own_k[b, :, cols], own_v[b, :, cols], None, True)
    else:
        top_s[...] = jnp.full_like(top_s[...], 2 * MASKED)
        sum_s[...] = jnp.zeros_like(sum_s[...])
        acc_s[...] = jnp.zeros_like(acc_s[...])
    for copy in copies:
        copy.wait()

    def loop(i, _):
        rows = pl.ds(pl.multiple_of(i * chunk, chunk), chunk)
        for b in range(branches):
            start = q_ref[b, FRAME_TOK:, :1].astype(jnp.float32)[:1]
            bias = jnp.where(frame_ref[pl.ds(i, 1), :] >= start, 0.0, MASKED)
            for h in range(HERE):
                cols = slice(h * HDIM, (h + 1) * HDIM)
                block_step(b, h, kv[0, rows, cols], kv[1, rows, cols], bias, False)
        return 0

    lax.fori_loop(0, blocks * 512 // chunk, loop, 0)
    lane = lax.broadcasted_iota(jnp.int32, (FRAME_TOK, HDIM), 1)
    for b in range(branches):
        stats = jnp.zeros((FRAME_TOK, HDIM), jnp.float32)
        for h in range(HERE):
            total = jnp.sum(sum_s[b, h], axis=1, keepdims=True)
            o_ref[b, :, h * HDIM : (h + 1) * HDIM] = (acc_s[b, h] / total).astype(o_ref.dtype)
            left = top_s[b, h] + jnp.log2(total)
            for part in range(3):
                piece = left.astype(jnp.bfloat16).astype(jnp.float32)
                stats = jnp.where(lane == h * 3 + part, piece, stats)
                left = left - piece
        if own:
            outs[1][b] = stats.astype(jnp.bfloat16)
        else:
            o_ref[b, :, WIDTH:] = stats.astype(jnp.bfloat16)


def attend(q, frames, parts, own=None):
    branches, blocks, chunk = q.shape[0], len(parts), 2048
    state = pltpu.VMEM((branches, HERE, FRAME_TOK, HDIM), jnp.float32)
    return pl.pallas_call(
        functools.partial(attend_kernel, branches, chunk, blocks, own is not None),
        out_shape=(
            jax.ShapeDtypeStruct((branches, FRAME_TOK, WIDTH), jnp.float32),
            jax.ShapeDtypeStruct((branches, FRAME_TOK, HDIM), jnp.bfloat16),
        )
        if own
        else jax.ShapeDtypeStruct((branches, FRAME_TOK, WIDTH + HDIM), jnp.bfloat16),
        in_specs=[VMEM, VMEM] + ([VMEM, VMEM] if own else []) + [ANY] * blocks,
        out_specs=(VMEM, VMEM) if own else VMEM,
        scratch_shapes=[
            pltpu.VMEM((2, blocks * 512, WIDTH), jnp.bfloat16),
            state,
            state,
            state,
            pltpu.SemaphoreType.DMA((blocks,)),
        ],
        compiler_params=pltpu.CompilerParams(vmem_limit_bytes=40 << 20),
        cost_estimate=pl.CostEstimate(
            flops=8 * branches * FRAME_TOK * blocks * 512 * WIDTH,
            bytes_accessed=blocks * 512 * WIDTH * 4,
            transcendentals=branches * FRAME_TOK * blocks * 512 * HERE,
        ),
    )(q, frames.reshape(-1, chunk), *(own or ()), *parts)


def merge_kernel(*refs):
    here, there = refs[-2:]
    packed = refs[-3]
    count = (len(refs) - 3) // 2
    for b in range(count):
        o_ref, stat_ref = refs[2 * b : 2 * b + 2]
        for h in range(HERE):
            cols = slice(h * HDIM, (h + 1) * HDIM)
            own = stat_ref[0, :, h * 3 : h * 3 + 3].astype(jnp.float32)
            far = packed[b, :, WIDTH + h * 3 : WIDTH + h * 3 + 3].astype(jnp.float32)
            own = jnp.sum(own, axis=1, keepdims=True)
            far = jnp.sum(far, axis=1, keepdims=True)
            top = jnp.maximum(own, far)
            own, far = jnp.exp2(own - top), jnp.exp2(far - top)
            scale = 1.0 / (own + far)
            o = (
                o_ref[0, :, cols] * (own * scale)
                + packed[b, :, cols].astype(jnp.float32) * (far * scale)
            ).astype(jnp.bfloat16)
            here[b, :, cols] = o[:128]
            there[b, :, cols] = o[128:]


def merge(parts, packed):
    out = jax.ShapeDtypeStruct((len(parts), 128, WIDTH), jnp.bfloat16)
    flat = [a for part in parts for a in part]
    return pl.pallas_call(
        merge_kernel,
        out_shape=(out, out),
        in_specs=[VMEM] * (len(flat) + 1),
        out_specs=(VMEM, VMEM),
        compiler_params=pltpu.CompilerParams(vmem_limit_bytes=24 << 20),
    )(*flat, packed)


def out_kernel(core, a_ref, b_ref, wa_ref, *rest):
    pieces, outs, w = rest[:4], rest[4:-1], rest[-1]
    count, depth = pieces[0].shape[0], wa_ref.shape[0]
    w[:depth] = wa_ref[...]
    for j, ref in enumerate(pieces):
        side = core[0] if j < 2 else 1 - core[0]
        at = depth + (side * 2 + j % 2) * count
        w[pl.ds(pl.multiple_of(at, 16), count)] = ref[...]
    rows, branches = a_ref.shape[1], range(a_ref.shape[0])
    x = jnp.concatenate(
        [jnp.concatenate([ref[b] for b in branches], axis=0) for ref in (a_ref, b_ref)], axis=1
    )
    o = jnp.dot(x, w[...], preferred_element_type=jnp.float32).astype(jnp.bfloat16)
    for b in range(a_ref.shape[0]):
        for j, ref in enumerate(outs):
            ref[b] = o[b * rows + j * 32 : b * rows + (j + 1) * 32]


def project_out(core, a, b, wa, pieces):
    branches, rows, width, block = a.shape[0], a.shape[1], wa.shape[1], 512
    count = rows // 32
    return pl.pallas_call(
        out_kernel,
        grid=(width // block,),
        out_shape=(jax.ShapeDtypeStruct((branches, 32, width), jnp.bfloat16),) * count,
        in_specs=[
            SMEM,
            pl.BlockSpec((branches, rows, WIDTH), lambda i: (0, 0, 0)),
            pl.BlockSpec((branches, rows, WIDTH), lambda i: (0, 0, 0)),
            pl.BlockSpec((WIDTH, block), lambda i: (0, i)),
        ]
        + [pl.BlockSpec((WIDTH // 4, block), lambda i: (0, i))] * 4,
        out_specs=(pl.BlockSpec((branches, 32, block), lambda i: (0, 0, i)),) * count,
        scratch_shapes=[pltpu.VMEM((2 * WIDTH, block), jnp.bfloat16)],
        compiler_params=pltpu.CompilerParams(vmem_limit_bytes=24 << 20),
        cost_estimate=pl.CostEstimate(
            flops=4 * branches * rows * WIDTH * width,
            bytes_accessed=4 * WIDTH * width + 2 * branches * rows * width,
            transcendentals=0,
        ),
    )(core, a, b, wa, *pieces)


def add(a, b):
    return (a.astype(jnp.float32) + b.astype(jnp.float32)).astype(jnp.bfloat16)


def shards(x, actions, visible_from, table, w_qkv, w_out, ctx):
    branch = lax.axis_index("branch")
    core, base = branch % 2, branch // 8 * 8
    hidden, gate, *quarters = norm(actions, x, jnp.transpose(table, (1, 0, 2)), w_out)
    w = jnp.transpose(w_qkv, (1, 0, 2))

    a0 = hidden
    a1, a3, b0 = turned(a0, "y", 1), turned(a0, "y", -1), along_seq(a0, 0, 1)
    a2 = turned(a1, "y", 1)
    b1, b3 = turned(b0, "y", 1), turned(b0, "y", -1)
    b2 = along_seq(a2, 0, 1)

    near = across_z(quarters[0])
    b2, near = lax.optimization_barrier((b2, near))
    far = along_branch(near, 0, 0, 1)

    ctx, _ = lax.optimization_barrier((ctx, hidden))
    c1 = turned(ctx, "x", 1)
    c3 = turned(ctx, "x", -1)
    c2 = turned(c1, "x", 1)
    mine = [ctx, c1, c3, c2]
    parts = list(mine)
    for part in mine:
        part, _ = lax.optimization_barrier((part, b0))
        parts.append(along_branch(part, 0, 0, 1))
    at = branch // 2 % 4
    order = []
    for c in (core, 1 - core):
        for d in (0, 2 * c - 1, 1 - 2 * c, 2):
            order.append(base + (at + d + 4) % 4 * 2 + c)
    frames = jnp.stack(order)[:, None] * 2 + jnp.arange(512, dtype=jnp.int32) // FRAME_TOK
    frames = frames.astype(jnp.float32)

    first = project_qkv([a0, a1, a3, b0], w)
    second = project_qkv([a2, b1, b3, b2], w)
    start = jnp.broadcast_to(visible_from.astype(jnp.bfloat16)[:, None, None], (2, 16, WIDTH))
    q, k, v = (
        jnp.concatenate([f[:, :96], s[:, :32], f[:, 96:], s[:, 32:]] + tail, axis=1)
        for f, s, tail in zip(first, second, ([start], [], []))
    )
    far_q = along_branch(q, 0, 1)
    quarter, _ = lax.optimization_barrier((quarters[1], b2))
    near_1 = across_z(quarter)
    o_0, s_0 = attend(q[:1], frames, parts, (k[:1], v[:1]))
    far_q, _ = lax.optimization_barrier((far_q, s_0))
    far_0 = attend(far_q[:1], frames, parts)
    packed_0 = along_branch(far_0, 0, 1)
    far_q, _ = lax.optimization_barrier((far_q[1:], far_0))
    far_1 = attend(far_q, frames, parts)
    packed_1 = along_branch(far_1, 0, 1)
    packed_0, _ = lax.optimization_barrier((packed_0, far_1))
    here_0, there_0 = merge([(o_0, s_0)], packed_0)
    other_0 = along_seq(there_0, 0, 1)
    last, _ = lax.optimization_barrier((q[1:], there_0))
    o_1, s_1 = attend(last, frames, parts, (k[1:], v[1:]))
    near_1, packed_1, o_1, other_0 = lax.optimization_barrier((near_1, packed_1, o_1, other_0))
    pieces = [near, near_1, far, along_branch(near_1, 0, 0, 1)]
    here_1, there_1 = merge([(o_1, s_1)], packed_1)
    other_1 = along_seq(there_1, 0, 1)

    core = core.astype(jnp.int32).reshape(1)
    here_0, _ = lax.optimization_barrier((here_0, there_1))
    p0, p1, p3, p2 = project_out(core, here_0, other_0, w_out, pieces)
    back, t3 = turned(p2, "y", -1), turned(p3, "y", 1)
    other_1, _ = lax.optimization_barrier((other_1, p0))
    r0, r1, r3, r2 = project_out(core, here_1, other_1, w_out, pieces)
    t1 = turned(add(p1, back), "y", -1)
    back, u3 = turned(r2, "y", -1), turned(r3, "y", 1)
    u1 = turned(add(r1, back), "y", -1)
    p0, t1, t3 = (jnp.concatenate(pair, 0) for pair in ((p0, r0), (t1, u1), (t3, u3)))
    sums = p0.astype(jnp.float32) + t1.astype(jnp.float32) + t3.astype(jnp.float32)
    return (x.astype(jnp.float32) + gate * sums).astype(jnp.bfloat16)


def solution(mesh):
    in_specs = (
        P("branch", "seq", None),
        P("branch"),
        P("branch"),
        P(),
        P(None, None, "seq"),
        P("seq", None),
        P(None, "branch", "seq"),
    )
    out_specs = P("branch", "seq", None)
    return jax.shard_map(shards, mesh=mesh, in_specs=in_specs, out_specs=out_specs, check_vma=False)
```

```python
import functools
import math

import jax
import jax.numpy as jnp
from jax import lax
from jax.experimental import pallas as pl
from jax.experimental.pallas import tpu as pltpu
from jax.sharding import PartitionSpec as P

HDIM = 128
ACTIONS = 16
FRAME_TOK = 256
HERE = 3
WIDTH = HERE * HDIM
SCALE2 = math.log2(math.e) * HDIM ** (-0.5)
MASKED = -1e30
VMEM = pl.BlockSpec(memory_space=pltpu.VMEM)
SMEM = pl.BlockSpec(memory_space=pltpu.SMEM)
ANY = pl.BlockSpec(memory_space=pl.ANY)


def along_seq(a, dy=0, dz=0):
    perm = [
        (z * 4 + y, (z + dz) % 2 * 4 + (y + dy) % 4) for z in range(2) for y in range(4)
    ]
    return lax.ppermute(a, "seq", perm)


def along_branch(a, dx=0, dz=0, dc=0):
    perm = [
        ((z * 4 + x) * 2 + c, ((z + dz) % 2 * 4 + (x + dx) % 4) * 2 + (c + dc) % 2)
        for z in range(2)
        for x in range(4)
        for c in range(2)
    ]
    return lax.ppermute(a, "branch", perm)


def turned(a, axis, step):
    perm = []
    for b in range(16):
        for s in range(8):
            way = step if b % 2 == 0 else -step
            z, x, y = b // 8 * 8, b // 2 % 4, s % 4
            if axis == "x":
                to = (z + (x + way) % 4 * 2 + b % 2, s)
            else:
                to = (b, s - y + (y + way) % 4)
            perm.append((b * 8 + s, to[0] * 8 + to[1]))
    return lax.ppermute(a, ("branch", "seq"), perm)


def across_z(a):
    perm = []
    for b in range(16):
        for s in range(8):
            perm.append((b * 8 + s, (b + 8) % 16 * 8 + (s + 4) % 8))
    return lax.ppermute(a, ("branch", "seq"), perm)


def norm_kernel(
    actions, x_hbm, table_hbm, w_hbm, hidden_ref, gate_ref, w_0, w_1, w_2, x_ref, table_ref, sems
):
    at = lax.rem(lax.axis_index("branch"), 2) * (w_hbm.shape[0] // 2)
    cuts = []
    for ref in (w_0, w_1, w_2):
        cuts.append(pl.ds(pl.multiple_of(at, 16), ref.shape[0]))
        at = at + ref.shape[0]
    copies = [
        pltpu.make_async_copy(x_hbm, x_ref, sems.at[0]),
        pltpu.make_async_copy(table_hbm, table_ref, sems.at[1]),
        pltpu.make_async_copy(w_hbm.at[cuts[0]], w_0, sems.at[2]),
        pltpu.make_async_copy(w_hbm.at[cuts[1]], w_1, sems.at[3]),
        pltpu.make_async_copy(w_hbm.at[cuts[2]], w_2, sems.at[4]),
    ]
    for copy in copies:
        copy.start()
    copies[0].wait()
    copies[1].wait()
    rows = lax.broadcasted_iota(jnp.int32, (ACTIONS, 1), 0)
    for b in range(x_ref.shape[0]):
        pick = rows == actions[b]
        shift, scale, gate = (
            jnp.sum(
                jnp.where(pick, table_ref[c].astype(jnp.float32), 0.0), axis=0, keepdims=True
            )
            for c in range(3)
        )
        gate_ref[b] = gate
        x = x_ref[b].astype(jnp.float32)
        centred = x - jnp.mean(x, axis=-1, keepdims=True)
        variance = jnp.mean(centred * centred, axis=-1, keepdims=True)
        normed = centred * (1.0 / jnp.sqrt(variance + 1e-06))
        hidden_ref[b] = (normed * (1.0 + scale) + shift).astype(jnp.bfloat16)
    copies[2].wait()
    copies[3].wait()
    copies[4].wait()


def norm(actions, x, table, w_out):
    rows, width = w_out.shape
    cuts = [
        jax.ShapeDtypeStruct((rows // part, width), w_out.dtype) for part in (4, 8, 8)
    ]
    return pl.pallas_call(
        norm_kernel,
        out_shape=(
            jax.ShapeDtypeStruct(x.shape, jnp.bfloat16),
            jax.ShapeDtypeStruct((x.shape[0], 1, x.shape[2]), jnp.float32),
            *cuts,
        ),
        in_specs=[SMEM, ANY, ANY, ANY],
        out_specs=(VMEM,) * 5,
        scratch_shapes=[
            pltpu.VMEM(x.shape, x.dtype),
            pltpu.VMEM(table.shape, table.dtype),
            pltpu.SemaphoreType.DMA((5,)),
        ],
        compiler_params=pltpu.CompilerParams(vmem_limit_bytes=56 << 20),
    )(actions, x, table, w_out)


def qkv_kernel(count, *refs):
    shards, w_ref, outs, acc = refs[:count], refs[count], refs[count + 1 : count + 4], refs[-1]
    step = pl.program_id(0)
    x = jnp.concatenate([s[b] for b in range(2) for s in shards], axis=0)

    @pl.when(step == 0)
    def _():
        acc[...] = jnp.zeros_like(acc)

    for c in range(3):
        acc[c] += jnp.dot(x, w_ref[c], preferred_element_type=jnp.float32)

    @pl.when(step == pl.num_programs(0) - 1)
    def _():
        rows = count * 32
        for c in range(3):
            for b in range(2):
                outs[c][b] = acc[c, b * rows : (b + 1) * rows].astype(jnp.bfloat16)


def project_qkv(shards, w):
    count, depth, block = len(shards), w.shape[1], 2560
    rows = count * 32
    out = jax.ShapeDtypeStruct((2, rows, WIDTH), jnp.bfloat16)
    return pl.pallas_call(
        functools.partial(qkv_kernel, count),
        grid=(depth // block,),
        out_shape=(out,) * 3,
        in_specs=[pl.BlockSpec((2, 32, block), lambda i: (0, 0, i))] * count
        + [pl.BlockSpec((3, block, WIDTH), lambda i: (0, i, 0))],
        out_specs=(pl.BlockSpec((2, rows, WIDTH), lambda i: (0, 0, 0)),) * 3,
        scratch_shapes=[pltpu.VMEM((3, 2 * rows, WIDTH), jnp.float32)],
        compiler_params=pltpu.CompilerParams(vmem_limit_bytes=32 << 20),
        cost_estimate=pl.CostEstimate(
            flops=2 * 2 * rows * depth * 3 * WIDTH,
            bytes_accessed=depth * 3 * WIDTH * 2 + 2 * rows * depth * 2,
            transcendentals=0,
        ),
    )(*shards, w)


def attend_kernel(branches, chunk, blocks, own, q_ref, frame_ref, *rest):
    if own:
        own_k, own_v, rest = rest[0], rest[1], rest[2:]
    parts, outs, (kv, top_s, sum_s, acc_s, sems) = rest[:blocks], rest[blocks:-5], rest[-5:]
    o_ref = outs[0]
    copies = [
        pltpu.make_async_copy(parts[i], kv.at[:, pl.ds(i * 512, 512)], sems.at[i])
        for i in range(blocks)
    ]
    for copy in copies:
        copy.start()

    def block_step(b, h, k, v, bias, first):
        q = q_ref[b, :FRAME_TOK, h * HDIM : (h + 1) * HDIM]
        s = lax.dot_general(q, k, (((1,), (1,)), ((), ())), preferred_element_type=jnp.float32)
        s = s * SCALE2
        if bias is not None:
            s = s + bias
        top = jnp.max(s, axis=1, keepdims=True)
        if first:
            new = jnp.broadcast_to(top, (FRAME_TOK, HDIM))
        else:
            old = top_s[b, h]
            new = jnp.maximum(old, top)
        p = jnp.exp2(s - new[:, :1])
        sums = p[:, :HDIM]
        for j in range(1, p.shape[1] // HDIM):
            sums = sums + p[:, j * HDIM : (j + 1) * HDIM]
        pv = jnp.dot(p.astype(jnp.bfloat16), v, preferred_element_type=jnp.float32)
        if first:
            sum_s[b, h] = sums
            acc_s[b, h] = pv
        else:
            factor = jnp.exp2(old - new)
            sum_s[b, h] = sum_s[b, h] * factor + sums
            acc_s[b, h] = acc_s[b, h] * factor + pv
        top_s[b, h] = new

    if own:
        for b in range(branches):
            for h in range(HERE):
                cols = slice(h * HDIM, (h + 1) * HDIM)
                block_step(b, h, own_k[b, :, cols], own_v[b, :, cols], None, True)
    else:
        top_s[...] = jnp.full_like(top_s[...], 2 * MASKED)
        sum_s[...] = jnp.zeros_like(sum_s[...])
        acc_s[...] = jnp.zeros_like(acc_s[...])
    for copy in copies:
        copy.wait()

    def loop(i, _):
        rows = pl.ds(pl.multiple_of(i * chunk, chunk), chunk)
        for b in range(branches):
            start = q_ref[b, FRAME_TOK:, :1].astype(jnp.float32)[:1]
            bias = jnp.where(frame_ref[pl.ds(i, 1), :] >= start, 0.0, MASKED)
            for h in range(HERE):
                cols = slice(h * HDIM, (h + 1) * HDIM)
                block_step(b, h, kv[0, rows, cols], kv[1, rows, cols], bias, False)
        return 0

    lax.fori_loop(0, blocks * 512 // chunk, loop, 0)
    lane = lax.broadcasted_iota(jnp.int32, (FRAME_TOK, HDIM), 1)
    for b in range(branches):
        stats = jnp.zeros((FRAME_TOK, HDIM), jnp.float32)
        for h in range(HERE):
            total = jnp.sum(sum_s[b, h], axis=1, keepdims=True)
            o_ref[b, :, h * HDIM : (h + 1) * HDIM] = (acc_s[b, h] / total).astype(o_ref.dtype)
            left = top_s[b, h] + jnp.log2(total)
            for part in range(3):
                piece = left.astype(jnp.bfloat16).astype(jnp.float32)
                stats = jnp.where(lane == h * 3 + part, piece, stats)
                left = left - piece
        if own:
            outs[1][b] = stats.astype(jnp.bfloat16)
        else:
            o_ref[b, :, WIDTH:] = stats.astype(jnp.bfloat16)


def attend(q, frames, parts, own=None):
    branches, blocks, chunk = q.shape[0], len(parts), 2048
    state = pltpu.VMEM((branches, HERE, FRAME_TOK, HDIM), jnp.float32)
    return pl.pallas_call(
        functools.partial(attend_kernel, branches, chunk, blocks, own is not None),
        out_shape=(
            jax.ShapeDtypeStruct((branches, FRAME_TOK, WIDTH), jnp.float32),
            jax.ShapeDtypeStruct((branches, FRAME_TOK, HDIM), jnp.bfloat16),
        )
        if own
        else jax.ShapeDtypeStruct((branches, FRAME_TOK, WIDTH + HDIM), jnp.bfloat16),
        in_specs=[VMEM, VMEM] + ([VMEM, VMEM] if own else []) + [ANY] * blocks,
        out_specs=(VMEM, VMEM) if own else VMEM,
        scratch_shapes=[
            pltpu.VMEM((2, blocks * 512, WIDTH), jnp.bfloat16),
            state,
            state,
            state,
            pltpu.SemaphoreType.DMA((blocks,)),
        ],
        compiler_params=pltpu.CompilerParams(vmem_limit_bytes=40 << 20),
        cost_estimate=pl.CostEstimate(
            flops=8 * branches * FRAME_TOK * blocks * 512 * WIDTH,
            bytes_accessed=blocks * 512 * WIDTH * 4,
            transcendentals=branches * FRAME_TOK * blocks * 512 * HERE,
        ),
    )(q, frames.reshape(-1, chunk), *(own or ()), *parts)


def merge_kernel(*refs):
    here, there = refs[-2:]
    packed = refs[-3]
    count = (len(refs) - 3) // 2
    for b in range(count):
        o_ref, stat_ref = refs[2 * b : 2 * b + 2]
        for h in range(HERE):
            cols = slice(h * HDIM, (h + 1) * HDIM)
            own = stat_ref[0, :, h * 3 : h * 3 + 3].astype(jnp.float32)
            far = packed[b, :, WIDTH + h * 3 : WIDTH + h * 3 + 3].astype(jnp.float32)
            own = jnp.sum(own, axis=1, keepdims=True)
            far = jnp.sum(far, axis=1, keepdims=True)
            top = jnp.maximum(own, far)
            own, far = jnp.exp2(own - top), jnp.exp2(far - top)
            scale = 1.0 / (own + far)
            o = (
                o_ref[0, :, cols] * (own * scale)
                + packed[b, :, cols].astype(jnp.float32) * (far * scale)
            ).astype(jnp.bfloat16)
            here[b, :, cols] = o[:128]
            there[b, :, cols] = o[128:]


def merge(parts, packed):
    out = jax.ShapeDtypeStruct((len(parts), 128, WIDTH), jnp.bfloat16)
    flat = [a for part in parts for a in part]
    return pl.pallas_call(
        merge_kernel,
        out_shape=(out, out),
        in_specs=[VMEM] * (len(flat) + 1),
        out_specs=(VMEM, VMEM),
        compiler_params=pltpu.CompilerParams(vmem_limit_bytes=24 << 20),
    )(*flat, packed)


def out_kernel(core, a_ref, b_ref, wa_ref, *rest):
    pieces, outs, w = rest[:6], rest[6:-1], rest[-1]
    depth = wa_ref.shape[0]
    w[:depth] = wa_ref[...]
    for side, refs in ((core[0], pieces[:3]), (1 - core[0], pieces[3:])):
        at = depth + side * (depth // 2)
        for ref in refs:
            w[pl.ds(pl.multiple_of(at, 16), ref.shape[0])] = ref[...]
            at = at + ref.shape[0]
    rows, branches = a_ref.shape[1], range(a_ref.shape[0])
    x = jnp.concatenate(
        [jnp.concatenate([ref[b] for b in branches], axis=0) for ref in (a_ref, b_ref)], axis=1
    )
    o = jnp.dot(x, w[...], preferred_element_type=jnp.float32).astype(jnp.bfloat16)
    for b in range(a_ref.shape[0]):
        for j, ref in enumerate(outs):
            ref[b] = o[b * rows + j * 32 : b * rows + (j + 1) * 32]


def project_out(core, a, b, wa, pieces):
    branches, rows, width, block = a.shape[0], a.shape[1], wa.shape[1], 1280
    count = rows // 32
    return pl.pallas_call(
        out_kernel,
        grid=(width // block,),
        out_shape=(jax.ShapeDtypeStruct((branches, 32, width), jnp.bfloat16),) * count,
        in_specs=[
            SMEM,
            pl.BlockSpec((branches, rows, WIDTH), lambda i: (0, 0, 0)),
            pl.BlockSpec((branches, rows, WIDTH), lambda i: (0, 0, 0)),
            pl.BlockSpec((WIDTH, block), lambda i: (0, i)),
        ]
        + [pl.BlockSpec((piece.shape[0], block), lambda i: (0, i)) for piece in pieces],
        out_specs=(pl.BlockSpec((branches, 32, block), lambda i: (0, 0, i)),) * count,
        scratch_shapes=[pltpu.VMEM((2 * WIDTH, block), jnp.bfloat16)],
        compiler_params=pltpu.CompilerParams(vmem_limit_bytes=24 << 20),
        cost_estimate=pl.CostEstimate(
            flops=4 * branches * rows * WIDTH * width,
            bytes_accessed=4 * WIDTH * width + 2 * branches * rows * width,
            transcendentals=0,
        ),
    )(core, a, b, wa, *pieces)


def add(a, b):
    return (a.astype(jnp.float32) + b.astype(jnp.float32)).astype(jnp.bfloat16)


def shards(x, actions, visible_from, table, w_qkv, w_out, ctx):
    branch = lax.axis_index("branch")
    core, base = branch % 2, branch // 8 * 8
    hidden, gate, *cuts = norm(actions, x, jnp.transpose(table, (1, 0, 2)), w_out)
    w = jnp.transpose(w_qkv, (1, 0, 2))

    a0 = hidden
    a1, a3, b0 = turned(a0, "y", 1), turned(a0, "y", -1), along_seq(a0, 0, 1)
    a2 = turned(a1, "y", 1)
    b1, b3 = turned(b0, "y", 1), turned(b0, "y", -1)
    b2 = along_seq(a2, 0, 1)

    near = across_z(cuts[0])
    b2, near = lax.optimization_barrier((b2, near))
    far = along_branch(near, 0, 0, 1)

    ctx, _ = lax.optimization_barrier((ctx, hidden))
    c1 = turned(ctx, "x", 1)
    c3 = turned(ctx, "x", -1)
    c2 = turned(c1, "x", 1)
    mine = [ctx, c1, c3, c2]
    parts = list(mine)
    for part in mine:
        part, _ = lax.optimization_barrier((part, b0))
        parts.append(along_branch(part, 0, 0, 1))
    at = branch // 2 % 4
    order = []
    for c in (core, 1 - core):
        for d in (0, 2 * c - 1, 1 - 2 * c, 2):
            order.append(base + (at + d + 4) % 4 * 2 + c)
    frames = jnp.stack(order)[:, None] * 2 + jnp.arange(512, dtype=jnp.int32) // FRAME_TOK
    frames = frames.astype(jnp.float32)

    first = project_qkv([a0, a1, a3, b0], w)
    second = project_qkv([a2, b1, b3, b2], w)
    start = jnp.broadcast_to(visible_from.astype(jnp.bfloat16)[:, None, None], (2, 16, WIDTH))
    q, k, v = (
        jnp.concatenate([f[:, :96], s[:, :32], f[:, 96:], s[:, 32:]] + tail, axis=1)
        for f, s, tail in zip(first, second, ([start], [], []))
    )
    far_q = along_branch(q, 0, 1)
    cut_1, cut_2, _ = lax.optimization_barrier((cuts[1], cuts[2], b2))
    near_1, near_2 = across_z(cut_1), along_seq(cut_2, 0, 1)
    o_0, s_0 = attend(q[:1], frames, parts, (k[:1], v[:1]))
    far_q, _ = lax.optimization_barrier((far_q, s_0))
    far_0 = attend(far_q[:1], frames, parts)
    packed_0 = along_branch(far_0, 0, 1)
    far_q, _ = lax.optimization_barrier((far_q[1:], far_0))
    far_1 = attend(far_q, frames, parts)
    packed_1 = along_branch(far_1, 0, 1)
    packed_0, _ = lax.optimization_barrier((packed_0, far_1))
    here_0, there_0 = merge([(o_0, s_0)], packed_0)
    other_0 = along_seq(there_0, 0, 1)
    last, _ = lax.optimization_barrier((q[1:], there_0))
    o_1, s_1 = attend(last, frames, parts, (k[1:], v[1:]))
    near_1, near_2, packed_1, o_1, other_0 = lax.optimization_barrier(
        (near_1, near_2, packed_1, o_1, other_0)
    )
    far_1, far_2 = along_branch(near_1, 0, 0, 1), along_branch(near_2, 0, 0, 1)
    pieces = [near, near_1, near_2, far, far_1, far_2]
    here_1, there_1 = merge([(o_1, s_1)], packed_1)
    other_1 = along_seq(there_1, 0, 1)

    core = core.astype(jnp.int32).reshape(1)
    here_0, _ = lax.optimization_barrier((here_0, there_1))
    p0, p1, p3, p2 = project_out(core, here_0, other_0, w_out, pieces)
    back, t3 = turned(p2, "y", -1), turned(p3, "y", 1)
    other_1, _ = lax.optimization_barrier((other_1, p0))
    r0, r1, r3, r2 = project_out(core, here_1, other_1, w_out, pieces)
    t1 = turned(add(p1, back), "y", -1)
    back, u3 = turned(r2, "y", -1), turned(r3, "y", 1)
    u1 = turned(add(r1, back), "y", -1)
    p0, t1, t3 = (jnp.concatenate(pair, 0) for pair in ((p0, r0), (t1, u1), (t3, u3)))
    sums = p0.astype(jnp.float32) + t1.astype(jnp.float32) + t3.astype(jnp.float32)
    return (x.astype(jnp.float32) + gate * sums).astype(jnp.bfloat16)


def solution(mesh):
    in_specs = (
        P("branch", "seq", None),
        P("branch"),
        P("branch"),
        P(),
        P(None, None, "seq"),
        P("seq", None),
        P(None, "branch", "seq"),
    )
    out_specs = P("branch", "seq", None)
    return jax.shard_map(shards, mesh=mesh, in_specs=in_specs, out_specs=out_specs, check_vma=False)
```

```python
import functools
import math

import jax
import jax.numpy as jnp
from jax import lax
from jax.experimental import pallas as pl
from jax.experimental.pallas import tpu as pltpu
from jax.sharding import PartitionSpec as P

HDIM = 128
ACTIONS = 16
FRAME_TOK = 256
HERE = 3
WIDTH = HERE * HDIM
SCALE2 = math.log2(math.e) * HDIM ** (-0.5)
MASKED = -1e30
VMEM = pl.BlockSpec(memory_space=pltpu.VMEM)
SMEM = pl.BlockSpec(memory_space=pltpu.SMEM)
ANY = pl.BlockSpec(memory_space=pl.ANY)


def along_seq(a, dy=0, dz=0):
    perm = [
        (z * 4 + y, (z + dz) % 2 * 4 + (y + dy) % 4) for z in range(2) for y in range(4)
    ]
    return lax.ppermute(a, "seq", perm)


def along_branch(a, dx=0, dz=0, dc=0):
    perm = [
        ((z * 4 + x) * 2 + c, ((z + dz) % 2 * 4 + (x + dx) % 4) * 2 + (c + dc) % 2)
        for z in range(2)
        for x in range(4)
        for c in range(2)
    ]
    return lax.ppermute(a, "branch", perm)


def turned(a, axis, step):
    perm = []
    for b in range(16):
        for s in range(8):
            way = step if b % 2 == 0 else -step
            z, x, y = b // 8 * 8, b // 2 % 4, s % 4
            if axis == "x":
                to = (z + (x + way) % 4 * 2 + b % 2, s)
            else:
                to = (b, s - y + (y + way) % 4)
            perm.append((b * 8 + s, to[0] * 8 + to[1]))
    return lax.ppermute(a, ("branch", "seq"), perm)


def across_z(a):
    perm = []
    for b in range(16):
        for s in range(8):
            perm.append((b * 8 + s, (b + 8) % 16 * 8 + (s + 4) % 8))
    return lax.ppermute(a, ("branch", "seq"), perm)


def norm_kernel(
    actions, x_hbm, table_hbm, w_hbm, hidden_ref, gate_ref, w_0, w_1, w_2, x_ref, table_ref, sems
):
    at = lax.rem(lax.axis_index("branch"), 2) * (w_hbm.shape[0] // 2)
    cuts = []
    for ref in (w_0, w_1, w_2):
        cuts.append(pl.ds(pl.multiple_of(at, 16), ref.shape[0]))
        at = at + ref.shape[0]
    copies = [
        pltpu.make_async_copy(x_hbm, x_ref, sems.at[0]),
        pltpu.make_async_copy(table_hbm, table_ref, sems.at[1]),
        pltpu.make_async_copy(w_hbm.at[cuts[0]], w_0, sems.at[2]),
        pltpu.make_async_copy(w_hbm.at[cuts[1]], w_1, sems.at[3]),
        pltpu.make_async_copy(w_hbm.at[cuts[2]], w_2, sems.at[4]),
    ]
    for copy in copies:
        copy.start()
    copies[0].wait()
    copies[1].wait()
    rows = lax.broadcasted_iota(jnp.int32, (ACTIONS, 1), 0)
    for b in range(x_ref.shape[0]):
        pick = rows == actions[b]
        shift, scale, gate = (
            jnp.sum(
                jnp.where(pick, table_ref[c].astype(jnp.float32), 0.0), axis=0, keepdims=True
            )
            for c in range(3)
        )
        gate_ref[b] = gate
        x = x_ref[b].astype(jnp.float32)
        centred = x - jnp.mean(x, axis=-1, keepdims=True)
        variance = jnp.mean(centred * centred, axis=-1, keepdims=True)
        normed = centred * (1.0 / jnp.sqrt(variance + 1e-06))
        hidden_ref[b] = (normed * (1.0 + scale) + shift).astype(jnp.bfloat16)
    copies[2].wait()
    copies[3].wait()
    copies[4].wait()


def norm(actions, x, table, w_out):
    rows, width = w_out.shape
    cuts = [
        jax.ShapeDtypeStruct((rows // part, width), w_out.dtype) for part in (4, 8, 8)
    ]
    return pl.pallas_call(
        norm_kernel,
        out_shape=(
            jax.ShapeDtypeStruct(x.shape, jnp.bfloat16),
            jax.ShapeDtypeStruct((x.shape[0], 1, x.shape[2]), jnp.float32),
            *cuts,
        ),
        in_specs=[SMEM, ANY, ANY, ANY],
        out_specs=(VMEM,) * 5,
        scratch_shapes=[
            pltpu.VMEM(x.shape, x.dtype),
            pltpu.VMEM(table.shape, table.dtype),
            pltpu.SemaphoreType.DMA((5,)),
        ],
        compiler_params=pltpu.CompilerParams(vmem_limit_bytes=56 << 20),
    )(actions, x, table, w_out)


def qkv_kernel(count, *refs):
    shards, w_ref, outs, acc = refs[:count], refs[count], refs[count + 1 : count + 4], refs[-1]
    step = pl.program_id(0)
    x = jnp.concatenate([s[b] for b in range(2) for s in shards], axis=0)

    @pl.when(step == 0)
    def _():
        acc[...] = jnp.zeros_like(acc)

    for c in range(3):
        acc[c] += jnp.dot(x, w_ref[c], preferred_element_type=jnp.float32)

    @pl.when(step == pl.num_programs(0) - 1)
    def _():
        rows = count * 32
        for c in range(3):
            for b in range(2):
                outs[c][b] = acc[c, b * rows : (b + 1) * rows].astype(jnp.bfloat16)


def project_qkv(shards, w):
    count, depth, block = len(shards), w.shape[1], 2560
    rows = count * 32
    out = jax.ShapeDtypeStruct((2, rows, WIDTH), jnp.bfloat16)
    return pl.pallas_call(
        functools.partial(qkv_kernel, count),
        grid=(depth // block,),
        out_shape=(out,) * 3,
        in_specs=[pl.BlockSpec((2, 32, block), lambda i: (0, 0, i))] * count
        + [pl.BlockSpec((3, block, WIDTH), lambda i: (0, i, 0))],
        out_specs=(pl.BlockSpec((2, rows, WIDTH), lambda i: (0, 0, 0)),) * 3,
        scratch_shapes=[pltpu.VMEM((3, 2 * rows, WIDTH), jnp.float32)],
        compiler_params=pltpu.CompilerParams(vmem_limit_bytes=32 << 20),
        cost_estimate=pl.CostEstimate(
            flops=2 * 2 * rows * depth * 3 * WIDTH,
            bytes_accessed=depth * 3 * WIDTH * 2 + 2 * rows * depth * 2,
            transcendentals=0,
        ),
    )(*shards, w)


def attend_kernel(branches, chunk, blocks, own, q_ref, frame_ref, *rest):
    if own:
        own_k, own_v, rest = rest[0], rest[1], rest[2:]
    parts, outs, (kv, top_s, sum_s, acc_s, sems) = rest[:blocks], rest[blocks:-5], rest[-5:]
    o_ref = outs[0]
    copies = [
        pltpu.make_async_copy(parts[i], kv.at[:, pl.ds(i * 512, 512)], sems.at[i])
        for i in range(blocks)
    ]
    for copy in copies:
        copy.start()

    def block_step(b, h, k, v, bias, first):
        q = q_ref[b, :FRAME_TOK, h * HDIM : (h + 1) * HDIM]
        s = lax.dot_general(q, k, (((1,), (1,)), ((), ())), preferred_element_type=jnp.float32)
        s = s * SCALE2
        if bias is not None:
            s = s + bias
        top = jnp.max(s, axis=1, keepdims=True)
        if first:
            new = jnp.broadcast_to(top, (FRAME_TOK, HDIM))
        else:
            old = top_s[b, h]
            new = jnp.maximum(old, top)
        p = jnp.exp2(s - new[:, :1])
        sums = p[:, :HDIM]
        for j in range(1, p.shape[1] // HDIM):
            sums = sums + p[:, j * HDIM : (j + 1) * HDIM]
        pv = jnp.dot(p.astype(jnp.bfloat16), v, preferred_element_type=jnp.float32)
        if first:
            sum_s[b, h] = sums
            acc_s[b, h] = pv
        else:
            factor = jnp.exp2(old - new)
            sum_s[b, h] = sum_s[b, h] * factor + sums
            acc_s[b, h] = acc_s[b, h] * factor + pv
        top_s[b, h] = new

    if own:
        for b in range(branches):
            for h in range(HERE):
                cols = slice(h * HDIM, (h + 1) * HDIM)
                block_step(b, h, own_k[b, :, cols], own_v[b, :, cols], None, True)
    else:
        top_s[...] = jnp.full_like(top_s[...], 2 * MASKED)
        sum_s[...] = jnp.zeros_like(sum_s[...])
        acc_s[...] = jnp.zeros_like(acc_s[...])
    for copy in copies:
        copy.wait()

    def loop(i, _):
        rows = pl.ds(pl.multiple_of(i * chunk, chunk), chunk)
        for b in range(branches):
            start = q_ref[b, FRAME_TOK:, :1].astype(jnp.float32)[:1]
            bias = jnp.where(frame_ref[pl.ds(i, 1), :] >= start, 0.0, MASKED)
            for h in range(HERE):
                cols = slice(h * HDIM, (h + 1) * HDIM)
                block_step(b, h, kv[0, rows, cols], kv[1, rows, cols], bias, False)
        return 0

    lax.fori_loop(0, blocks * 512 // chunk, loop, 0)
    lane = lax.broadcasted_iota(jnp.int32, (FRAME_TOK, HDIM), 1)
    for b in range(branches):
        stats = jnp.zeros((FRAME_TOK, HDIM), jnp.float32)
        for h in range(HERE):
            total = jnp.sum(sum_s[b, h], axis=1, keepdims=True)
            o_ref[b, :, h * HDIM : (h + 1) * HDIM] = (acc_s[b, h] / total).astype(o_ref.dtype)
            left = top_s[b, h] + jnp.log2(total)
            for part in range(3):
                piece = left.astype(jnp.bfloat16).astype(jnp.float32)
                stats = jnp.where(lane == h * 3 + part, piece, stats)
                left = left - piece
        if own:
            outs[1][b] = stats.astype(jnp.bfloat16)
        else:
            o_ref[b, :, WIDTH:] = stats.astype(jnp.bfloat16)


def attend(q, frames, parts, own=None):
    branches, blocks, chunk = q.shape[0], len(parts), 4096
    state = pltpu.VMEM((branches, HERE, FRAME_TOK, HDIM), jnp.float32)
    return pl.pallas_call(
        functools.partial(attend_kernel, branches, chunk, blocks, own is not None),
        out_shape=(
            jax.ShapeDtypeStruct((branches, FRAME_TOK, WIDTH), jnp.float32),
            jax.ShapeDtypeStruct((branches, FRAME_TOK, HDIM), jnp.bfloat16),
        )
        if own
        else jax.ShapeDtypeStruct((branches, FRAME_TOK, WIDTH + HDIM), jnp.bfloat16),
        in_specs=[VMEM, VMEM] + ([VMEM, VMEM] if own else []) + [ANY] * blocks,
        out_specs=(VMEM, VMEM) if own else VMEM,
        scratch_shapes=[
            pltpu.VMEM((2, blocks * 512, WIDTH), jnp.bfloat16),
            state,
            state,
            state,
            pltpu.SemaphoreType.DMA((blocks,)),
        ],
        compiler_params=pltpu.CompilerParams(vmem_limit_bytes=40 << 20),
        cost_estimate=pl.CostEstimate(
            flops=8 * branches * FRAME_TOK * blocks * 512 * WIDTH,
            bytes_accessed=blocks * 512 * WIDTH * 4,
            transcendentals=branches * FRAME_TOK * blocks * 512 * HERE,
        ),
    )(q, frames.reshape(-1, chunk), *(own or ()), *parts)


def merge_kernel(*refs):
    here, there = refs[-2:]
    packed = refs[-3]
    count = (len(refs) - 3) // 2
    for b in range(count):
        o_ref, stat_ref = refs[2 * b : 2 * b + 2]
        for h in range(HERE):
            cols = slice(h * HDIM, (h + 1) * HDIM)
            own = stat_ref[0, :, h * 3 : h * 3 + 3].astype(jnp.float32)
            far = packed[b, :, WIDTH + h * 3 : WIDTH + h * 3 + 3].astype(jnp.float32)
            own = jnp.sum(own, axis=1, keepdims=True)
            far = jnp.sum(far, axis=1, keepdims=True)
            top = jnp.maximum(own, far)
            own, far = jnp.exp2(own - top), jnp.exp2(far - top)
            scale = 1.0 / (own + far)
            o = (
                o_ref[0, :, cols] * (own * scale)
                + packed[b, :, cols].astype(jnp.float32) * (far * scale)
            ).astype(jnp.bfloat16)
            here[b, :, cols] = o[:128]
            there[b, :, cols] = o[128:]


def merge(parts, packed):
    out = jax.ShapeDtypeStruct((len(parts), 128, WIDTH), jnp.bfloat16)
    flat = [a for part in parts for a in part]
    return pl.pallas_call(
        merge_kernel,
        out_shape=(out, out),
        in_specs=[VMEM] * (len(flat) + 1),
        out_specs=(VMEM, VMEM),
        compiler_params=pltpu.CompilerParams(vmem_limit_bytes=24 << 20),
    )(*flat, packed)


def out_kernel(core, a_ref, b_ref, wa_ref, *rest):
    pieces, outs, w = rest[:6], rest[6:-1], rest[-1]
    depth = wa_ref.shape[0]
    w[:depth] = wa_ref[...]
    for side, refs in ((core[0], pieces[:3]), (1 - core[0], pieces[3:])):
        at = depth + side * (depth // 2)
        for ref in refs:
            w[pl.ds(pl.multiple_of(at, 16), ref.shape[0])] = ref[...]
            at = at + ref.shape[0]
    rows, branches = a_ref.shape[1], range(a_ref.shape[0])
    x = jnp.concatenate(
        [jnp.concatenate([ref[b] for b in branches], axis=0) for ref in (a_ref, b_ref)], axis=1
    )
    o = jnp.dot(x, w[...], preferred_element_type=jnp.float32).astype(jnp.bfloat16)
    for b in range(a_ref.shape[0]):
        for j, ref in enumerate(outs):
            ref[b] = o[b * rows + j * 32 : b * rows + (j + 1) * 32]


def project_out(core, a, b, wa, pieces):
    branches, rows, width, block = a.shape[0], a.shape[1], wa.shape[1], 2560
    count = rows // 32
    return pl.pallas_call(
        out_kernel,
        grid=(width // block,),
        out_shape=(jax.ShapeDtypeStruct((branches, 32, width), jnp.bfloat16),) * count,
        in_specs=[
            SMEM,
            pl.BlockSpec((branches, rows, WIDTH), lambda i: (0, 0, 0)),
            pl.BlockSpec((branches, rows, WIDTH), lambda i: (0, 0, 0)),
            pl.BlockSpec((WIDTH, block), lambda i: (0, i)),
        ]
        + [pl.BlockSpec((piece.shape[0], block), lambda i: (0, i)) for piece in pieces],
        out_specs=(pl.BlockSpec((branches, 32, block), lambda i: (0, 0, i)),) * count,
        scratch_shapes=[pltpu.VMEM((2 * WIDTH, block), jnp.bfloat16)],
        compiler_params=pltpu.CompilerParams(vmem_limit_bytes=24 << 20),
        cost_estimate=pl.CostEstimate(
            flops=4 * branches * rows * WIDTH * width,
            bytes_accessed=4 * WIDTH * width + 2 * branches * rows * width,
            transcendentals=0,
        ),
    )(core, a, b, wa, *pieces)


def add(a, b):
    return (a.astype(jnp.float32) + b.astype(jnp.float32)).astype(jnp.bfloat16)


def shards(x, actions, visible_from, table, w_qkv, w_out, ctx):
    branch = lax.axis_index("branch")
    core, base = branch % 2, branch // 8 * 8
    hidden, gate, *cuts = norm(actions, x, jnp.transpose(table, (1, 0, 2)), w_out)
    w = jnp.transpose(w_qkv, (1, 0, 2))

    a0 = hidden
    a1, a3, b0 = turned(a0, "y", 1), turned(a0, "y", -1), along_seq(a0, 0, 1)
    a2 = turned(a1, "y", 1)
    b1, b3 = turned(b0, "y", 1), turned(b0, "y", -1)
    b2 = along_seq(a2, 0, 1)

    near = across_z(cuts[0])
    b2, near = lax.optimization_barrier((b2, near))
    far = along_branch(near, 0, 0, 1)

    ctx, _ = lax.optimization_barrier((ctx, hidden))
    c1 = turned(ctx, "x", 1)
    c3 = turned(ctx, "x", -1)
    c2 = turned(c1, "x", 1)
    mine = [ctx, c1, c3, c2]
    parts = list(mine)
    for part in mine:
        part, _ = lax.optimization_barrier((part, b0))
        parts.append(along_branch(part, 0, 0, 1))
    at = branch // 2 % 4
    order = []
    for c in (core, 1 - core):
        for d in (0, 2 * c - 1, 1 - 2 * c, 2):
            order.append(base + (at + d + 4) % 4 * 2 + c)
    frames = jnp.stack(order)[:, None] * 2 + jnp.arange(512, dtype=jnp.int32) // FRAME_TOK
    frames = frames.astype(jnp.float32)

    first = project_qkv([a0, a1, a3, b0], w)
    second = project_qkv([a2, b1, b3, b2], w)
    start = jnp.broadcast_to(visible_from.astype(jnp.bfloat16)[:, None, None], (2, 16, WIDTH))
    q, k, v = (
        jnp.concatenate([f[:, :96], s[:, :32], f[:, 96:], s[:, 32:]] + tail, axis=1)
        for f, s, tail in zip(first, second, ([start], [], []))
    )
    far_q = along_branch(q, 0, 1)
    cut_1, cut_2, _ = lax.optimization_barrier((cuts[1], cuts[2], b2))
    near_1, near_2 = across_z(cut_1), along_seq(cut_2, 0, 1)
    o_0, s_0 = attend(q[:1], frames, parts, (k[:1], v[:1]))
    far_q, _ = lax.optimization_barrier((far_q, s_0))
    far_0 = attend(far_q[:1], frames, parts)
    packed_0 = along_branch(far_0, 0, 1)
    far_q, _ = lax.optimization_barrier((far_q[1:], far_0))
    far_1 = attend(far_q, frames, parts)
    packed_1 = along_branch(far_1, 0, 1)
    packed_0, _ = lax.optimization_barrier((packed_0, far_1))
    here_0, there_0 = merge([(o_0, s_0)], packed_0)
    other_0 = along_seq(there_0, 0, 1)
    last, _ = lax.optimization_barrier((q[1:], there_0))
    o_1, s_1 = attend(last, frames, parts, (k[1:], v[1:]))
    near_1, near_2, packed_1, o_1, other_0 = lax.optimization_barrier(
        (near_1, near_2, packed_1, o_1, other_0)
    )
    far_1, far_2 = along_branch(near_1, 0, 0, 1), along_branch(near_2, 0, 0, 1)
    pieces = [near, near_1, near_2, far, far_1, far_2]
    here_1, there_1 = merge([(o_1, s_1)], packed_1)
    other_1 = along_seq(there_1, 0, 1)

    core = core.astype(jnp.int32).reshape(1)
    here_0, _ = lax.optimization_barrier((here_0, there_1))
    p0, p1, p3, p2 = project_out(core, here_0, other_0, w_out, pieces)
    back, t3 = turned(p2, "y", -1), turned(p3, "y", 1)
    other_1, _ = lax.optimization_barrier((other_1, p0))
    r0, r1, r3, r2 = project_out(core, here_1, other_1, w_out, pieces)
    t1 = turned(add(p1, back), "y", -1)
    back, u3 = turned(r2, "y", -1), turned(r3, "y", 1)
    u1 = turned(add(r1, back), "y", -1)
    p0, t1, t3 = (jnp.concatenate(pair, 0) for pair in ((p0, r0), (t1, u1), (t3, u3)))
    sums = p0.astype(jnp.float32) + t1.astype(jnp.float32) + t3.astype(jnp.float32)
    return (x.astype(jnp.float32) + gate * sums).astype(jnp.bfloat16)


def solution(mesh):
    in_specs = (
        P("branch", "seq", None),
        P("branch"),
        P("branch"),
        P(),
        P(None, None, "seq"),
        P("seq", None),
        P(None, "branch", "seq"),
    )
    out_specs = P("branch", "seq", None)
    return jax.shard_map(shards, mesh=mesh, in_specs=in_specs, out_specs=out_specs, check_vma=False)
```
